512 devices in a mesh: segment: 8 (over z), tok: 64 (over x, y, core).
Axes of the slice: x: 4, y: 8, z: 8, core: 2. Of those that a mesh axis runs over, the one named last changes fastest.
Arguments:
- inputs: bfloat16 [16384, 768], P('tok'), may hold values from -6 to 6
- keys: bfloat16 [8, 16384, 768], P('segment', 'tok'), may hold values from -6 to 6
- values: bfloat16 [8, 16384, 768], P('segment', 'tok'), may hold values from -8 to 8
- rates: float32 [8, 16384], P('segment', 'tok'), may hold values from 0.0002 to 0.003
- gains: float32 [8, 768], P('segment'), may hold values from 0.1 to 1.9
- w_in: bfloat16 [8, 384, 2, 768], P('segment', 'tok'), may hold values from -0.21875 to 0.21875
- w_out: bfloat16 [8, 768, 384], P('segment', 'tok'), may hold values from -0.3125 to 0.3125
Outputs:
- layer_outputs: bfloat16 [8, 16384, 768], P('segment', 'tok')
The draws below stay inside these ranges and needn't reach their ends.
All inputs are finite; a program needn't handle non-finite values.
Results may differ from the reference program's by a relative error of at most 0.028.
Values may be sent and summed in bfloat16 or wider, within the bound.
A program may use at most 64 MiB of HBM per device.

```python
import math
import jax
import jax.numpy as jnp
from jax import lax

HD = 768
FH = 384
TOKENS = 16384
SEGMENTS = 8


def spiked(drawn, key, source, target, parts, factor):
    owner, partner = [(jnp.arange(drawn.shape[position]) // (drawn.shape[position] // parts)).reshape([-1 if axis == position else 1 for axis in range(drawn.ndim)]) for position in (source, target)]
    chosen = jax.random.permutation(key, parts)[partner]
    strong = (owner == chosen) | (owner == (partner + parts // 2) % parts)
    return jnp.where(strong, factor * drawn, drawn)


def shard_levels(stream_key, extent, shards, smallest, largest):
    def one(axis_at, parts):
        steps = jax.random.uniform(jax.random.fold_in(jax.random.fold_in(stream_key, 6), axis_at), (parts,), jnp.float32, smallest / len(shards), largest / len(shards))
        return jnp.repeat(jnp.exp(steps), extent[axis_at] // parts).reshape((-1,) + (1,) * (len(extent) - axis_at - 1))

    factor_of = one(*shards[0])
    for cut in shards[1:]:
        factor_of = factor_of * one(*cut)
    return factor_of


def noise(own_key, extent, width, most, cuts=(), held_as=jnp.bfloat16):
    loudness = shard_levels(own_key, extent, cuts, -0.22, 0.18) if cuts else 1.0
    result = jax.random.normal(own_key, extent, jnp.float32) * width * loudness
    return jnp.minimum(jnp.maximum(result, -most), most).astype(held_as)


def heavy_noise(stream_key, dims, scale, most, pieces, heavy, kind=jnp.bfloat16):
    drawn = scale * jax.random.normal(stream_key, dims, jnp.float32)
    if pieces:
        drawn = drawn * shard_levels(stream_key, dims, pieces, -0.22, 0.18)
    return jnp.clip(spiked(drawn, jax.random.fold_in(stream_key, 3), *heavy), -most, most).astype(kind)


def setup_inputs(seed: int = 0) -> dict:
    arg_keys = jax.random.split(jax.random.key(seed), 8)
    return {
        "inputs": noise(arg_keys[0], (TOKENS, HD), 1.0, 6.0, ((0, 64),)),
        "keys": noise(arg_keys[1], (SEGMENTS, TOKENS, HD), 1.0, 6.0, ((0, 8), (1, 64))),
        "values": heavy_noise(arg_keys[2], (SEGMENTS, TOKENS, HD), 1.0, 8.0, ((0, 8), (1, 64)), (1, 2, 64, 4.0)),
        "rates": jnp.clip(jnp.exp(math.log(0.003) - 2.7080502 * jax.random.uniform(arg_keys[3], (SEGMENTS, TOKENS), jnp.float32) ** shard_levels(arg_keys[3], (SEGMENTS, TOKENS), ((0, 8), (1, 64)), -0.2, 0.2)), 0.0002, 0.003),
        "gains": jnp.clip(1.0 + 0.18 * jax.random.normal(arg_keys[4], (SEGMENTS, HD), jnp.float32), 0.1, 1.9),
        "w_in": noise(arg_keys[5], (SEGMENTS, FH, 2, HD), HD ** -0.5, 0.21875, ((0, 8), (1, 64))),
        "w_out": noise(arg_keys[6], (SEGMENTS, HD, FH), FH ** -0.5, 0.3125, ((0, 8), (1, 64))),
    }


def renorm(weight, gradient):
    base = weight.astype(jnp.float32)
    moved = base + gradient
    base_rms = jnp.sqrt(lax.optimization_barrier(jnp.mean(base * base, axis=-1, keepdims=True)) + 1e-06)
    moved_rms = jnp.sqrt(lax.optimization_barrier(jnp.mean(moved * moved, axis=-1, keepdims=True)) + 1e-06)
    return (moved * (base_rms / moved_rms)).astype(jnp.bfloat16)

def apply_layer(rows_in, gain_row, fast_in, fast_out):
    rows32 = rows_in.astype(jnp.float32)
    scale = jax.lax.rsqrt(lax.optimization_barrier(jnp.mean(rows32 * rows32, axis=-1, keepdims=True)) + 1e-06)
    normed = (rows32 * scale * gain_row).astype(jnp.bfloat16)
    pre_act = jnp.einsum('td,fcd->tcf', normed.astype(jnp.float32), fast_in.astype(jnp.float32))
    gate_pre = pre_act[:, 0]
    mixed = (gate_pre * jax.nn.sigmoid(gate_pre) * pre_act[:, 1]).astype(jnp.bfloat16)
    branch = jnp.dot(mixed, fast_out.T, preferred_element_type=jnp.float32)
    return (rows32 + branch).astype(jnp.bfloat16)

def reference(inputs, keys, values, rates, gains, w_in, w_out):
    results = []
    current = inputs
    for layer_index in range(SEGMENTS):
        keys32 = keys[layer_index].astype(jnp.float32)
        hidden = jnp.einsum('td,fcd->tcf', keys32, w_in[layer_index].astype(jnp.float32))
        gate_pre = hidden[:, 0]
        up_pre = hidden[:, 1]
        sigmoid_h = jax.nn.sigmoid(gate_pre)
        silu_gate = gate_pre * sigmoid_h
        activation = (silu_gate * up_pre).astype(jnp.bfloat16)
        target = (rates[layer_index][:, None] * values[layer_index].astype(jnp.float32)).astype(jnp.bfloat16)
        d_act = jnp.dot(target, w_out[layer_index], preferred_element_type=jnp.float32)
        d_gate = d_act * up_pre * (sigmoid_h * (1.0 + gate_pre * (1.0 - sigmoid_h)))
        d_up = d_act * silu_gate
        d_hid = jnp.stack([d_gate, d_up], axis=1).astype(jnp.bfloat16)
        grad_in = jnp.einsum('tcf,td->fcd', d_hid.astype(jnp.float32), keys32)
        grad_out = jnp.dot(target.T, activation, preferred_element_type=jnp.float32)
        new_in = renorm(w_in[layer_index], grad_in)
        new_out = renorm(w_out[layer_index], grad_out)
        current = apply_layer(current, gains[layer_index], new_in, new_out)
        results.append(current)
    return jnp.stack(results)
```

```python
import functools

import jax
import jax.numpy as jnp
import numpy as np
from jax import lax
from jax.experimental import pallas as pl
from jax.experimental.pallas import tpu as pltpu
from jax.sharding import Mesh
from jax.sharding import PartitionSpec as P

NX, NY, NC, NZ = 4, 8, 2, 8
TOK = ("tok_0", "tok_1", "tok_2")
MESH = pl.DeviceIdType.MESH
F32 = jnp.float32
BF = jnp.bfloat16
HD, FH, ROWS = 768, 384, 256
PIECE = 16
GROUPS = ROWS // PIECE


def constants():
    c_in = np.zeros((96, 128), np.float32)
    for half in range(2):
        for y in range(NY):
            for r in range(6):
                c_in[half * 48 + y * 6 + r, y * 16 + r * 2 + half] = 1
    c_out = np.zeros((48, 64), np.float32)
    for x in range(NX):
        for r in range(12):
            c_out[x * 12 + r, x * 16 + r] = 1
    p_f = np.zeros((FH, FH), np.float32)
    for c in range(NC):
        for x in range(NX):
            for y in range(NY):
                for r in range(6):
                    p_f[((x * NY + y) * NC + c) * 6 + r, (c * NX + x) * 48 + y * 6 + r] = 1
    p_j = np.zeros((HD, HD), np.float32)
    for c in range(NC):
        for x in range(NX):
            for y in range(NY):
                for r in range(12):
                    p_j[((x * NY + y) * NC + c) * 12 + r, (c * NY + y) * 48 + x * 12 + r] = 1
    return [jnp.asarray(a, BF) for a in (c_in, c_out, p_f, p_j, p_j.T)]


def nt(a, b):
    return lax.dot_general(a, b, (((1,), (1,)), ((), ())), preferred_element_type=F32)


def nn(a, b):
    return lax.dot_general(a, b, (((1,), (0,)), ((), ())), preferred_element_type=F32)


def tn(a, b):
    return lax.dot_general(a, b, (((0,), (0,)), ((), ())), preferred_element_type=F32)


def renormed(base, gradient):
    moved = base + gradient
    base_rms = jnp.sqrt(jnp.mean(base * base, axis=-1, keepdims=True) + 1e-06)
    moved_rms = jnp.sqrt(jnp.mean(moved * moved, axis=-1, keepdims=True) + 1e-06)
    return (moved * (base_rms / moved_rms)).astype(BF)


def kernel(
    win_own, wout_own, rates, gains, c_in, c_out, p_f, keys_h, vals_h, inputs_h, pj_h, pjt_h,
    out,
    keys, vals, pj, pjt, rows_in,
    winpad, woutpad, win, wout,
    target_t, targetp_t, dact_t, dhid_t, act_t,
    gs_in, gs_out, gr_in, gr_out, gi, go,
    hx_s, hx_r, hy_s, hy_r, ky_s, ky_r, kx_s, kx_r,
    new_in, new_out,
    lsem, ya_s, ya_r, xa_s, xa_r, xb_s, xb_r, yb_s, yb_r, cb_s, cb_r, cc_s, cc_r,
    ri_s, ri_r, ro_s, ro_r, rx_s, rx_r, ry_s, ry_r, rky_s, rky_r, rkx_s, rkx_r,
    n1_s, n1_r, m1_s, m1_r, n2_s, n2_r, m2_s, m2_r, n3_s, n3_r, m3_s, m3_r,
    z_s, z_r,
):
    z = lax.axis_index("segment")
    x = lax.axis_index("tok_0")
    y = lax.axis_index("tok_1")
    c = lax.axis_index("tok_2")
    oc = 1 - c

    def ypeer(d):
        return lax.rem(y + d, NY)

    def xpeer(d):
        return lax.rem(x + d, NX)

    def at_y(d):
        return (z, x, ypeer(d), c)

    def at_x(d):
        return (z, xpeer(d), y, c)

    sibling = (z, x, y, oc)
    sent = []

    def remote(src, dst, ss, rs, dev):
        return pltpu.make_async_remote_copy(
            src_ref=src, dst_ref=dst, send_sem=ss, recv_sem=rs, device_id=dev, device_id_type=MESH
        )

    def send(src, dst, ss, rs, dev):
        cp = remote(src, dst, ss, rs, dev)
        cp.start()
        sent.append(cp)

    def arrived(dst, ss, rs, dev):
        remote(dst, dst, ss, rs, dev).wait_recv()

    local = [
        pltpu.make_async_copy(s, d, lsem.at[i])
        for i, (s, d) in enumerate(((vals_h, vals), (pjt_h, pjt), (keys_h, keys), (pj_h, pj)))
    ]
    for cp in local:
        cp.start()
    first = pltpu.make_async_copy(inputs_h, rows_in, lsem.at[4])

    @pl.when(z == 0)
    def _():
        first.start()

    bar = pltpu.get_barrier_semaphore()
    for d in range(1, NY):
        pl.semaphore_signal(bar, inc=1, device_id=at_y(d), device_id_type=MESH)
    for d in range(1, NX):
        pl.semaphore_signal(bar, inc=1, device_id=at_x(d), device_id_type=MESH)
    pl.semaphore_signal(bar, inc=1, device_id=sibling, device_id_type=MESH)
    for d in (1, NZ - 1):
        pl.semaphore_signal(bar, inc=1, device_id=(lax.rem(z + d, NZ), x, y, c), device_id_type=MESH)
    winpad[y] = win_own[...]
    woutpad[x] = nn(wout_own[...], p_f[...]).astype(BF)
    pl.semaphore_wait(bar, NY - 1 + NX - 1 + 1 + 2)

    for d in range(1, NX):
        send(woutpad.at[x], woutpad.at[x], xa_s.at[d], xa_r.at[d], at_x(d))
    for d in (4, 3, 5, 2, 6, 1, 7):
        send(winpad.at[y], winpad.at[y], ya_s.at[d], ya_r.at[d], at_y(d))

    local[0].wait()
    target_t[...] = (vals[...].astype(F32).T * rates[...]).astype(BF)
    for cp in local[1:]:
        cp.wait()
    targetp_t[...] = nn(pjt[...], target_t[...]).astype(BF)

    for d in range(1, NX):
        arrived(woutpad.at[xpeer(NX - d)], xa_s.at[d], xa_r.at[d], at_x(d))
    mine_o = c * NY + y
    wout[mine_o] = nn(c_out[...], woutpad[...].reshape(64, FH)).astype(BF)
    for d in (4, 3, 5, 2, 6, 1, 7):
        send(wout.at[mine_o], wout.at[mine_o], yb_s.at[d], yb_r.at[d], at_y(d))
    send(wout.at[mine_o], wout.at[mine_o], cc_s.at[0], cc_r.at[0], sibling)
    for d in (1, 7, 2, 6, 3, 5, 4):
        arrived(winpad.at[ypeer(NY - d)], ya_s.at[d], ya_r.at[d], at_y(d))
    mine_i = c * NX + x
    win[mine_i] = nn(c_in[...], winpad[...].reshape(128, HD)).astype(BF)
    for d in (2, 1, 3):
        send(win.at[mine_i], win.at[mine_i], xb_s.at[d], xb_r.at[d], at_x(d))
    send(win.at[mine_i], win.at[mine_i], cb_s.at[0], cb_r.at[0], sibling)
    for d in (1, 7, 2, 6, 3, 5, 4):
        slot = c * NY + ypeer(NY - d)
        arrived(wout.at[slot], yb_s.at[d], yb_r.at[d], at_y(d))
        send(wout.at[slot], wout.at[slot], cc_s.at[d], cc_r.at[d], sibling)
    for d in (1, 3, 2):
        slot = c * NX + xpeer(NX - d)
        arrived(win.at[slot], xb_s.at[d], xb_r.at[d], at_x(d))
        send(win.at[slot], win.at[slot], cb_s.at[d], cb_r.at[d], sibling)
    for d in range(NY):
        arrived(wout.at[oc * NY + ypeer(NY - d)], cc_s.at[d], cc_r.at[d], sibling)
    for d in range(NX):
        arrived(win.at[oc * NX + xpeer(NX - d)], cb_s.at[d], cb_r.at[d], sibling)

    dact_t[...] = tn(wout[...].reshape(HD, FH), targetp_t[...])

    def block(b, carry):
        hidden = nt(win[b], keys[...])
        gate = hidden[:48]
        up = hidden[48:]
        sig = jax.nn.sigmoid(gate)
        silu = gate * sig
        here = pl.ds(pl.multiple_of(b * 48, 16), 48)
        act_t[here, :] = (silu * up).astype(BF)
        da = dact_t[here, :]
        dhid_t[0, here, :] = (da * up * (sig * (1.0 + gate * (1.0 - sig)))).astype(BF)
        dhid_t[1, here, :] = (da * silu).astype(BF)
        return carry

    lax.fori_loop(0, NC * NX, block, 0)

    def out_rows(core):
        return pl.ds(pl.multiple_of(core * FH, FH), FH)

    gs_out[...] = nt(target_t[out_rows(oc), :], act_t[...]).astype(BF)
    send(gs_out, gr_out, ro_s, ro_r, sibling)
    order = (2, 1, 3, 0)

    def x_rows(d):
        return pl.ds(pl.multiple_of(xpeer(d) * 96, 32), 96)

    for d in order:
        gs_in[x_rows(d), :] = nn(dhid_t[oc, x_rows(d), :], keys[...]).astype(BF)
        send(gs_in.at[x_rows(d)], gr_in.at[x_rows(d)], ri_s.at[d], ri_r.at[d], sibling)
    go[...] = nt(target_t[out_rows(c), :], act_t[...])
    for d in order:
        gi[x_rows(d), :] = nn(dhid_t[c, x_rows(d), :], keys[...])
    arrived(gr_out, ro_s, ro_r, sibling)
    go[...] = go[...] + gr_out[...].astype(F32)

    def y_rows(d):
        return pl.ds(pl.multiple_of(ypeer(d) * 48, 16), 48)

    for d in (4, 3, 5, 2, 6, 1, 7):
        hy_s[ypeer(d)] = go[y_rows(d), :].astype(BF)
        send(hy_s.at[ypeer(d)], hy_r.at[y], ry_s.at[d], ry_r.at[d], at_y(d))
    for d in order:
        arrived(gr_in.at[x_rows(d)], ri_s.at[d], ri_r.at[d], sibling)
        total = gi[x_rows(d), :] + gr_in[x_rows(d), :].astype(F32)
        if d:
            hx_s[xpeer(d)] = total.astype(BF)
            send(hx_s.at[xpeer(d)], hx_r.at[x], rx_s.at[d], rx_r.at[d], at_x(d))
        else:
            gi[x_rows(0), :] = total

    total_o = go[y_rows(0), :]
    for d in (1, 7, 2, 6, 3, 5, 4):
        src = ypeer(NY - d)
        arrived(hy_r.at[src], ry_s.at[d], ry_r.at[d], at_y(d))
        total_o = total_o + hy_r[src].astype(F32)
    go[0:48, :] = total_o
    for k in range(3):
        kx_s[k] = total_o[k * 16 : k * 16 + 16].astype(BF)
    for d in range(1, NX):
        dest = xpeer(d)

        @pl.when(dest < 3)
        def _():
            remote(kx_s.at[dest], kx_r.at[x], rkx_s.at[d], rkx_r.at[d], at_x(d)).start()

    total_i = gi[x_rows(0), :]
    for d in (1, 3, 2):
        src = xpeer(NX - d)
        arrived(hx_r.at[src], rx_s.at[d], rx_r.at[d], at_x(d))
        total_i = total_i + hx_r[src].astype(F32)
    gi[0:96, :] = total_i
    for k in range(6):
        ky_s[k] = total_i[k * 16 : k * 16 + 16].astype(BF)
    for d in (4, 3, 5, 2, 6, 1, 7):
        dest = ypeer(d)

        @pl.when(dest < 6)
        def _():
            remote(ky_s.at[dest], ky_r.at[y], rky_s.at[d], rky_r.at[d], at_y(d)).start()

    row_o = pl.multiple_of(c * FH + y * 48 + x * 16, 16)

    @pl.when(x < 3)
    def _():
        g = go[pl.ds(pl.multiple_of(x * 16, 16), 16), :]
        for d in range(1, NX):
            src = xpeer(NX - d)
            arrived(kx_r.at[src], rkx_s.at[d], rkx_r.at[d], at_x(d))
            g = g + kx_r[src].astype(F32)
        base = nn(pj[pl.ds(row_o, 16), :], wout[...].reshape(HD, FH))
        new_out[pl.ds(row_o, 16), :] = renormed(base, g)
        for d in (2, 1, 3):
            here = new_out.at[pl.ds(row_o, 16)]
            remote(here, here, m1_s.at[d], m1_r.at[d], at_x(d)).start()

    row_i = pl.multiple_of(c * FH + x * 96 + y * 16, 16)

    @pl.when(y < 6)
    def _():
        g = gi[pl.ds(pl.multiple_of(y * 16, 16), 16), :]
        for d in (1, 7, 2, 6, 3, 5, 4):
            src = ypeer(NY - d)
            arrived(ky_r.at[src], rky_s.at[d], rky_r.at[d], at_y(d))
            g = g + ky_r[src].astype(F32)
        k = x * 6 + y
        b = k // 3
        start = pl.multiple_of(c * 48 + (k - b * 3) * 16, 16)
        base = win[b, pl.ds(start, 16), :].astype(F32)
        new_in[pl.ds(row_i, 16), :] = renormed(base, g)
        for d in (4, 3, 5, 2, 6, 1, 7):
            here = new_in.at[pl.ds(row_i, 16)]
            remote(here, here, n1_s.at[d], n1_r.at[d], at_y(d)).start()

    def out_block(core, yy):
        return new_out.at[pl.ds(pl.multiple_of(core * FH + yy * 48, 16), 48)]

    def in_block(core, xx):
        return new_in.at[pl.ds(pl.multiple_of(core * FH + xx * 96, 32), 96)]

    for d in range(1, NX):
        src = xpeer(NX - d)

        @pl.when(src < 3)
        def _():
            here = new_out.at[pl.ds(pl.multiple_of(c * FH + y * 48 + src * 16, 16), 16)]
            arrived(here, m1_s.at[d], m1_r.at[d], at_x(d))

    for d in (4, 3, 5, 2, 6, 1, 7):
        send(out_block(c, y), out_block(c, y), m2_s.at[d], m2_r.at[d], at_y(d))
    send(out_block(c, y), out_block(c, y), m3_s.at[0], m3_r.at[0], sibling)
    for d in (1, 7, 2, 6, 3, 5, 4):
        src = ypeer(NY - d)

        @pl.when(src < 6)
        def _():
            here = new_in.at[pl.ds(pl.multiple_of(c * FH + x * 96 + src * 16, 16), 16)]
            arrived(here, n1_s.at[d], n1_r.at[d], at_y(d))

    for d in (2, 1, 3):
        send(in_block(c, x), in_block(c, x), n2_s.at[d], n2_r.at[d], at_x(d))
    send(in_block(c, x), in_block(c, x), n3_s.at[0], n3_r.at[0], sibling)
    for d in (1, 7, 2, 6, 3, 5, 4):
        here = out_block(c, ypeer(NY - d))
        arrived(here, m2_s.at[d], m2_r.at[d], at_y(d))
        send(here, here, m3_s.at[d], m3_r.at[d], sibling)
    for d in (1, 3, 2):
        here = in_block(c, xpeer(NX - d))
        arrived(here, n2_s.at[d], n2_r.at[d], at_x(d))
        send(here, here, n3_s.at[d], n3_r.at[d], sibling)
    for d in range(NX):
        arrived(in_block(oc, xpeer(NX - d)), n3_s.at[d], n3_r.at[d], sibling)
    for d in range(NY):
        arrived(out_block(oc, ypeer(NY - d)), m3_s.at[d], m3_r.at[d], sibling)

    @pl.when(z == 0)
    def _():
        first.wait()

    after = (lax.rem(z + 1, NZ), x, y, c)

    def piece(g, carry):
        here = pl.ds(pl.multiple_of(g * PIECE, PIECE), PIECE)

        @pl.when(z > 0)
        def _():
            arrived(rows_in.at[here], z_s.at[g], z_r.at[g], after)

        rows32 = rows_in[here, :].astype(F32)
        scale = lax.rsqrt(jnp.mean(rows32 * rows32, axis=-1, keepdims=True) + 1e-06)
        normed = (rows32 * scale * gains[...]).astype(BF)
        pre = nt(normed, new_in[...])
        gate = pre[:, :FH]
        mixed = (gate * jax.nn.sigmoid(gate) * pre[:, FH:]).astype(BF)
        out[here, :] = (rows32 + nt(mixed, new_out[...])).astype(BF)

        @pl.when(z < NZ - 1)
        def _():
            remote(out.at[here], rows_in.at[here], z_s.at[g], z_r.at[g], after).start()

        return carry

    lax.fori_loop(0, GROUPS, piece, 0)

    for cp in sent:
        cp.wait_send()
    for d in range(1, NX):
        dest = xpeer(d)

        @pl.when(dest < 3)
        def _():
            remote(kx_s.at[dest], kx_r.at[x], rkx_s.at[d], rkx_r.at[d], at_x(d)).wait_send()

        @pl.when(x < 3)
        def _():
            here = new_out.at[pl.ds(row_o, 16)]
            remote(here, here, m1_s.at[d], m1_r.at[d], at_x(d)).wait_send()

    for d in range(1, NY):
        dest = ypeer(d)

        @pl.when(dest < 6)
        def _():
            remote(ky_s.at[dest], ky_r.at[y], rky_s.at[d], rky_r.at[d], at_y(d)).wait_send()

        @pl.when(y < 6)
        def _():
            here = new_in.at[pl.ds(row_i, 16)]
            remote(here, here, n1_s.at[d], n1_r.at[d], at_y(d)).wait_send()

    @pl.when(z < NZ - 1)
    def _():
        def left(g, carry):
            here = pl.ds(pl.multiple_of(g * PIECE, PIECE), PIECE)
            remote(out.at[here], rows_in.at[here], z_s.at[g], z_r.at[g], after).wait_send()
            return carry

        lax.fori_loop(0, GROUPS, left, 0)


def per_device(inputs, keys, values, rates, gains, w_in, w_out):
    win_own = jnp.pad(w_in.reshape(12, HD), ((0, 4), (0, 0)))
    wout_own = jnp.pad(w_out.reshape(12, FH), ((0, 4), (0, 0)))
    c_in, c_out, p_f, p_j, p_jt = constants()
    vm = pl.BlockSpec(memory_space=pltpu.VMEM)
    hb = pl.BlockSpec(memory_space=pl.ANY)
    V = pltpu.VMEM
    D = pltpu.SemaphoreType.DMA
    scratch = [
        V((ROWS, HD), BF), V((ROWS, HD), BF), V((HD, HD), BF), V((HD, HD), BF), V((ROWS, HD), BF),
        V((NY, 16, HD), BF), V((NX, 16, FH), BF), V((8, 96, HD), BF), V((16, 48, FH), BF),
        V((HD, ROWS), BF), V((HD, ROWS), BF), V((FH, ROWS), F32), V((2, FH, ROWS), BF), V((FH, ROWS), BF),
        V((FH, HD), BF), V((FH, FH), BF), V((FH, HD), BF), V((FH, FH), BF), V((FH, HD), F32), V((FH, FH), F32),
        V((NX, 96, HD), BF), V((NX, 96, HD), BF), V((NY, 48, FH), BF), V((NY, 48, FH), BF),
        V((6, 16, HD), BF), V((NY, 16, HD), BF), V((3, 16, FH), BF), V((NX, 16, FH), BF),
        V((HD, HD), BF), V((HD, FH), BF),
        D((5,)),
        D((NY,)), D((NY,)), D((NX,)), D((NX,)), D((NX,)), D((NX,)), D((NY,)), D((NY,)),
        D((NX,)), D((NX,)), D((NY,)), D((NY,)),
        D((NX,)), D((NX,)), D, D, D((NX,)), D((NX,)), D((NY,)), D((NY,)),
        D((NY,)), D((NY,)), D((NX,)), D((NX,)),
        D((NY,)), D((NY,)), D((NX,)), D((NX,)), D((NX,)), D((NX,)), D((NY,)), D((NY,)),
        D((NX,)), D((NX,)), D((NY,)), D((NY,)),
        D((GROUPS,)), D((GROUPS,)),
    ]
    result = pl.pallas_call(
        kernel,
        out_shape=jax.ShapeDtypeStruct((ROWS, HD), BF),
        in_specs=[vm] * 7 + [hb] * 5,
        out_specs=vm,
        scratch_shapes=scratch,
        compiler_params=pltpu.CompilerParams(
            collective_id=0, has_side_effects=True, vmem_limit_bytes=48 * 2**20
        ),
        cost_estimate=pl.CostEstimate(flops=1500000000, bytes_accessed=6000000, transcendentals=400000),
    )(win_own, wout_own, rates, gains, c_in, c_out, p_f, keys[0], values[0], inputs, p_j, p_jt)
    return result[None]


def solution(mesh):
    split = Mesh(
        mesh.devices.reshape(mesh.shape["segment"], NX, NY, NC), ("segment", "tok_0", "tok_1", "tok_2")
    )
    in_specs = (
        P(TOK, None),
        P("segment", TOK, None),
        P("segment", TOK, None),
        P("segment", TOK),
        P("segment", None),
        P("segment", TOK, None, None),
        P("segment", TOK, None),
    )
    return jax.shard_map(
        per_device, mesh=split, in_specs=in_specs, out_specs=P("segment", TOK, None), check_vma=False
    )
```

```python
import functools

import jax
import jax.numpy as jnp
import numpy as np
from jax import lax
from jax.experimental import pallas as pl
from jax.experimental.pallas import tpu as pltpu
from jax.sharding import Mesh
from jax.sharding import PartitionSpec as P

NX, NY, NC, NZ = 4, 8, 2, 8
TOK = ("tok_0", "tok_1", "tok_2")
MESH = pl.DeviceIdType.MESH
F32 = jnp.float32
BF = jnp.bfloat16
HD, FH, ROWS = 768, 384, 256
PIECE = 16
GROUPS = ROWS // PIECE


def constants():
    c_in = np.zeros((48, 64), np.float32)
    for half in range(2):
        for y in range(4):
            for r in range(6):
                c_in[half * 24 + y * 6 + r, y * 16 + r * 2 + half] = 1
    c_out = np.zeros((48, 64), np.float32)
    for x in range(NX):
        for r in range(12):
            c_out[x * 12 + r, x * 16 + r] = 1
    p_f = np.zeros((FH, FH), np.float32)
    for c in range(NC):
        for x in range(NX):
            for y in range(NY):
                for r in range(6):
                    p_f[((x * NY + y) * NC + c) * 6 + r, (c * NX + x) * 48 + y * 6 + r] = 1
    p_w = np.zeros((HD, HD), np.float32)
    for b in range(16):
        for half in range(2):
            for r in range(24):
                p_w[b * 48 + half * 24 + r, half * FH + b * 24 + r] = 1
    p_jt = np.zeros((HD, HD), np.float32)
    for c in range(NC):
        for x in range(NX):
            for y in range(NY):
                for r in range(12):
                    p_jt[(c * NY + y) * 48 + x * 12 + r, ((x * NY + y) * NC + c) * 12 + r] = 1
    return [jnp.asarray(a, BF) for a in (c_in, c_out, p_f, p_w, p_jt)]


def nt(a, b):
    return lax.dot_general(a, b, (((1,), (1,)), ((), ())), preferred_element_type=F32)


def nn(a, b):
    return lax.dot_general(a, b, (((1,), (0,)), ((), ())), preferred_element_type=F32)


def tn(a, b):
    return lax.dot_general(a, b, (((0,), (0,)), ((), ())), preferred_element_type=F32)


def parts(a):
    high = a.astype(BF)
    return high, (a - high.astype(F32)).astype(BF)


def row_squares(w):
    high, low = parts(w.astype(F32) * w.astype(F32))
    ones = jnp.ones((16, w.shape[1]), BF)
    return nt(ones, high) + nt(ones, low)


def moved_by(a, matrix):
    high, low = parts(a)
    return nn(high, matrix) + nn(low, matrix)


NEAR = (1, 7, 2, 6, 3, 5, 4)
FAR = (4, 3, 5, 2, 6, 1, 7)
STEPS = (4, 3, 5, 2, 6, 1, 7, 0)


def kernel(
    win_h, wout_h, rates_h, gains_h, cin_h, cout_h, pf_h, keys_h, vals_h, inputs_h, pw_h, pjt_h,
    out,
    win_own, wout_own, rates, gains, c_in, c_out, p_f, keys, vals, p_w, pjt, rows_in, pad32,
    winpad, woutpad, win, wout,
    keys_t, target_t, targetp_t, dact_t, dhid_t, act_t,
    gs, gr, half, hx_s, hx_r, hy_s, hy_r, ky_s, ky_r, kx_s, kx_r, own_sum, base_x, base_y, scale_in, scale_out,
    new, squares,
    lsem, ya_s, ya_r, xa_s, xa_r, xb_s, xb_r, yb_s, yb_r, cb_s, cb_r, cc_s, cc_r,
    rc_s, rc_r, rx_s, rx_r, ry_s, ry_r, rky_s, rky_r, rkx_s, rkx_r,
    n1_s, n1_r, m2_s, m2_r, n2_s, n2_r, n3_s, n3_r,
    z_s, z_r,
):
    z = lax.axis_index("segment")
    x = lax.axis_index("tok_0")
    y = lax.axis_index("tok_1")
    c = lax.axis_index("tok_2")
    oc = 1 - c

    def ypeer(d):
        return lax.rem(y + d, NY)

    def xpeer(d):
        return lax.rem(x + d, NX)

    def at_y(d):
        return (z, x, ypeer(d), c)

    def at_x(d):
        return (z, xpeer(d), y, c)

    sibling = (z, x, y, oc)
    later = []

    def remote(src, dst, ss, rs, dev):
        return pltpu.make_async_remote_copy(
            src_ref=src, dst_ref=dst, send_sem=ss, recv_sem=rs, device_id=dev, device_id_type=MESH
        )

    def send(src, dst, ss, rs, dev):
        cp = remote(src, dst, ss, rs, dev)
        cp.start()
        later.append(cp.wait_send)

    def send_if(cond, src, dst, ss, rs, dev):
        cp = remote(src, dst, ss, rs, dev)
        pl.when(cond)(cp.start)
        later.append(functools.partial(pl.when(cond), cp.wait_send))

    def arrived(dst, ss, rs, dev):
        remote(dst, dst, ss, rs, dev).wait_recv()

    pairs = (
        (win_h.at[0], win_own), (wout_h.at[0], wout_own), (pf_h, p_f), (vals_h.at[0], vals), (rates_h, rates),
        (pjt_h, pjt), (cin_h, c_in), (cout_h, c_out), (keys_h.at[0], keys), (pw_h, p_w), (gains_h, gains),
    )
    local = [pltpu.make_async_copy(s, d, lsem.at[i]) for i, (s, d) in enumerate(pairs)]
    for cp in local:
        cp.start()
    first = pltpu.make_async_copy(inputs_h, rows_in, lsem.at[len(pairs)])

    @pl.when(z == 0)
    def _():
        first.start()

    bar = pltpu.get_barrier_semaphore()
    for d in range(1, NY):
        pl.semaphore_signal(bar, inc=1, device_id=at_y(d), device_id_type=MESH)
    for d in range(1, NX):
        pl.semaphore_signal(bar, inc=1, device_id=at_x(d), device_id_type=MESH)
    pl.semaphore_signal(bar, inc=1, device_id=sibling, device_id_type=MESH)
    for d in (1, NZ - 1):
        pl.semaphore_signal(bar, inc=1, device_id=(lax.rem(z + d, NZ), x, y, c), device_id_type=MESH)
    pad32[...] = jnp.zeros_like(pad32)
    local[0].wait()
    for r in range(6):
        pad32[2 * r : 2 * r + 2, :] = win_own[r].astype(F32)
    winpad[y] = pad32[...].astype(BF)
    local[1].wait()
    local[2].wait()
    pad32[0:12, 0:FH] = wout_own[...].astype(F32)
    woutpad[x] = nn(pad32[:, 0:FH].astype(BF), p_f[...]).astype(BF)
    pl.semaphore_wait(bar, NY - 1 + NX - 1 + 1 + 2)

    for d in range(1, NX):
        send(woutpad.at[x], woutpad.at[x], xa_s.at[d], xa_r.at[d], at_x(d))
    group = y // 4
    place = y - group * 4

    def in_group(g, d):
        return g * 4 + lax.rem(place + d, 4)

    for g, ds in ((group, (2, 1, 3)), (1 - group, (0, 2, 1, 3))):
        for d in ds:
            to = in_group(g, d)
            send(winpad.at[y], winpad.at[y], ya_s.at[to], ya_r.at[y], (z, x, to, c))

    local[3].wait()
    local[4].wait()
    target_t[...] = (vals[...].astype(F32).T * rates[...]).astype(BF)
    for cp in local[5:]:
        cp.wait()

    for d in range(1, NX):
        arrived(woutpad.at[xpeer(NX - d)], xa_s.at[d], xa_r.at[d], at_x(d))
    mine_o = c * NY + y
    wout[mine_o] = nn(c_out[...], woutpad[...].reshape(64, FH)).astype(BF)
    for d in FAR:
        send(wout.at[mine_o], wout.at[mine_o], yb_s.at[d], yb_r.at[d], at_y(d))
    send(wout.at[mine_o], wout.at[mine_o], cc_s.at[0], cc_r.at[0], sibling)
    for n, (g, ds) in enumerate(((group, (1, 3, 2)), (1 - group, (0, 1, 3, 2)))):
        for d in ds:
            src = in_group(g, d)
            arrived(winpad.at[src], ya_s.at[src], ya_r.at[src], (z, x, src, c))
        mine_i = (c * NX + x) * 2 + g
        win[mine_i] = nn(c_in[...], winpad[pl.ds(g * 4, 4)].reshape(64, HD)).astype(BF)
        for d in (2, 1, 3):
            send(win.at[mine_i], win.at[mine_i], xb_s.at[n, d], xb_r.at[n, d], at_x(d))
        send(win.at[mine_i], win.at[mine_i], cb_s.at[n, 0], cb_r.at[n, 0], sibling)
        if n == 0:
            targetp_t[...] = nn(pjt[...], target_t[...]).astype(BF)
    keys_t[...] = keys[...].astype(F32).T.astype(BF)

    def win_slot(core, d, n):
        return win.at[(core * NX + xpeer(NX - d)) * 2 + (group if n == 0 else 1 - group)]

    for d in NEAR:
        slot = wout.at[c * NY + ypeer(NY - d)]
        arrived(slot, yb_s.at[d], yb_r.at[d], at_y(d))
        send(slot, slot, cc_s.at[d], cc_r.at[d], sibling)
    for n in range(2):
        for d in (1, 3, 2):
            slot = win_slot(c, d, n)
            arrived(slot, xb_s.at[n, d], xb_r.at[n, d], at_x(d))
            send(slot, slot, cb_s.at[n, d], cb_r.at[n, d], sibling)
    for d in range(NY):
        arrived(wout.at[oc * NY + ypeer(NY - d)], cc_s.at[d], cc_r.at[d], sibling)
    dact_t[...] = tn(wout[...].reshape(HD, FH), targetp_t[...])
    for n in range(2):
        for d in range(NX):
            arrived(win_slot(oc, d, n), cb_s.at[n, d], cb_r.at[n, d], sibling)

    def block(b, carry):
        hidden = nt(win[pl.ds(b * 2, 2)].reshape(96, HD), keys[...]).reshape(2, 2, 24, ROWS)
        gate = hidden[:, 0].reshape(48, ROWS)
        up = hidden[:, 1].reshape(48, ROWS)
        sig = jax.nn.sigmoid(gate)
        silu = gate * sig
        here = pl.ds(pl.multiple_of(b * 48, 16), 48)
        act_t[here, :] = (silu * up).astype(BF)
        da = dact_t[here, :]
        dhid_t[0, here, :] = (da * up * (sig * (1.0 + gate * (1.0 - sig)))).astype(BF)
        dhid_t[1, here, :] = (da * silu).astype(BF)
        return carry

    lax.fori_loop(0, NC * NX, block, 0)

    def out_part(core):
        return nt(act_t[pl.ds(pl.multiple_of(core * 192, 64), 192), :], target_t[...])

    def in_part(core):
        return nt(keys_t[pl.ds(pl.multiple_of(core * FH, FH), FH), :], dhid_t[...].reshape(HD, ROWS))

    def x_rows(d):
        return pl.ds(pl.multiple_of(xpeer(d) * 112, 16), 112)

    y_part = pl.ds(448, 128)
    gs[384:576, :] = out_part(oc).astype(BF)
    send(gs.at[y_part], gr.at[y_part], rc_s.at[4], rc_r.at[4], sibling)
    gs[0:384, :] = in_part(oc).astype(BF)
    for d in (2, 1, 3, 0):
        send(gs.at[x_rows(d)], gr.at[x_rows(d)], rc_s.at[d], rc_r.at[d], sibling)
    half[384:576, :] = out_part(c)
    half[0:384, :] = in_part(c)

    arrived(gr.at[y_part], rc_s.at[4], rc_r.at[4], sibling)
    for k in range(8):
        here = pl.ds(448 + k * 16, 16)
        total = half[here, :] + gr[here, :].astype(F32)
        half[here, :] = total
        hy_s[k] = total.astype(BF)
    for d in FAR:
        send(hy_s.at[ypeer(d)], hy_r.at[y], ry_s.at[d], ry_r.at[d], at_y(d))
    for d in (2, 1, 3, 0):
        arrived(gr.at[x_rows(d)], rc_s.at[d], rc_r.at[d], sibling)
        total = half[x_rows(d), :] + gr[x_rows(d), :].astype(F32)
        if d:
            hx_s[xpeer(d)] = total.reshape(7, 16, HD).astype(BF)
        else:
            half[x_rows(0), :] = total
    for r in STEPS:
        i = ypeer(r)
        for d in (2, 1, 3):
            send_if(i < 7, hx_s.at[xpeer(d), i], hx_r.at[x, i], rx_s.at[d, i], rx_r.at[d, i], at_x(d))

    def row_of(core, k):
        return pl.multiple_of(k * 16 + core * 384 + (k // 24) * (384 - core * 192), 16)

    lane_in = lax.broadcasted_iota(jnp.int32, (16, HD), 1) - lax.broadcasted_iota(jnp.int32, (16, HD), 0)
    lane_out = lax.broadcasted_iota(jnp.int32, (16, FH), 1) - lax.broadcasted_iota(jnp.int32, (16, FH), 0)

    def base_block(k, ref):
        @pl.when(k < 24)
        def _():
            pick = jnp.where(lane_in == row_of(c, k), 1.0, 0.0).astype(BF)
            ref[...] = nn(nt(pick, win[...].reshape(HD, HD)).astype(BF), p_w[...])

        @pl.when(k >= 24)
        def _():
            pick = jnp.where(lane_out == row_of(c, k) - HD, 1.0, 0.0).astype(BF)
            ref[...] = nn(nt(pick, wout[...].reshape(HD, FH)).astype(BF), pjt[...])

    mine_x = x * 7 + jnp.minimum(y, 6)
    mine_y = 28 + y
    base_block(mine_x, base_x)
    base_block(mine_y, base_y)
    scale_in[...] = jnp.sqrt(moved_by(row_squares(win[...].reshape(HD, HD)), p_w[...]) / HD + 1e-06)
    scale_out[...] = jnp.sqrt(moved_by(row_squares(wout[...].reshape(HD, FH)), pjt[...]) / FH + 1e-06)

    def reduce_step(r):
        i = ypeer(r)

        @pl.when(i < 7)
        def _():
            total = half[pl.ds(pl.multiple_of(x * 112 + i * 16, 16), 16), :]
            for d in (1, 3, 2):
                src = xpeer(NX - d)
                arrived(hx_r.at[src, i], rx_s.at[d, i], rx_r.at[d, i], at_x(d))
                total = total + hx_r[src, i].astype(F32)
            if r:
                ky_s[i] = total.astype(BF)
            else:
                own_sum[...] = total

        if r:
            send_if(i < 7, ky_s.at[i], ky_r.at[y], rky_s.at[r], rky_r.at[r], at_y(r))

    for r in STEPS[:4]:
        reduce_step(r)
    total = half[pl.ds(pl.multiple_of(448 + y * 16, 16), 16), :]
    for d in NEAR:
        src = ypeer(NY - d)
        arrived(hy_r.at[src], ry_s.at[d], ry_r.at[d], at_y(d))
        total = total + hy_r[src].astype(F32)
    kx_s[...] = total.astype(BF)
    for d in (2, 1, 3):
        send(kx_s, kx_r.at[x], rkx_s.at[d], rkx_r.at[d], at_x(d))
    base_y[...] = base_y[...] + total
    for r in STEPS[4:]:
        reduce_step(r)

    def new_block(core, k):
        return new.at[pl.ds(row_of(core, k), 16)]

    moved = base_y[...]
    for d in (1, 3, 2):
        src = xpeer(NX - d)
        arrived(kx_r.at[src], rkx_s.at[d], rkx_r.at[d], at_x(d))
        moved = moved + kx_r[src].astype(F32)
    mine = new_block(c, mine_y)
    mine[...] = moved.astype(BF)
    for d in FAR:
        send(mine, mine, m2_s.at[d], m2_r.at[d], at_y(d))
    send(mine, mine, n3_s.at[mine_y], n3_r.at[mine_y], sibling)

    mine = new_block(c, mine_x)

    @pl.when(y < 7)
    def _():
        moved = base_x[...] + own_sum[...]
        for d in NEAR:
            src = ypeer(NY - d)
            arrived(ky_r.at[src], rky_s.at[d], rky_r.at[d], at_y(d))
            moved = moved + ky_r[src].astype(F32)
        mine[...] = moved.astype(BF)

    def spread(cond, k, i):
        here = new_block(c, k)
        for d in (2, 1, 3):
            send_if(cond, here, here, n2_s.at[d, i], n2_r.at[d, i], at_x(d))
        send_if(cond, here, here, n3_s.at[k], n3_r.at[k], sibling)

    for d in FAR:
        send_if(y < 7, mine, mine, n1_s.at[d], n1_r.at[d], at_y(d))
    spread(y < 7, mine_x, jnp.minimum(y, 6))
    for d in NEAR:
        src = ypeer(NY - d)
        k = x * 7 + src

        @pl.when(src < 7)
        def _():
            arrived(new_block(c, k), n1_s.at[d], n1_r.at[d], at_y(d))

        spread(src < 7, k, src)
    for d in NEAR:
        k = 28 + ypeer(NY - d)
        here = new_block(c, k)
        arrived(here, m2_s.at[d], m2_r.at[d], at_y(d))
        send(here, here, n3_s.at[k], n3_r.at[k], sibling)
    for r in (0,) + NEAR:
        i = ypeer(NY - r)
        for d in (1, 3, 2):
            k = xpeer(NX - d) * 7 + i

            @pl.when(i < 7)
            def _():
                arrived(new_block(c, k), n2_s.at[d, i], n2_r.at[d, i], at_x(d))

            send_if(i < 7, new_block(c, k), new_block(c, k), n3_s.at[k], n3_r.at[k], sibling)

    squares[...] = jnp.zeros_like(squares)

    def add_squares(core, k):
        block = new_block(core, k)[...].astype(F32)
        squares[k // 24] = squares[k // 24] + block * block

    def own_squares(k, carry):
        add_squares(c, k)
        return carry

    def other_squares(k, carry):
        arrived(new_block(oc, k), n3_s.at[k], n3_r.at[k], sibling)
        add_squares(oc, k)
        return carry

    lax.fori_loop(0, 36, own_squares, 0)
    lax.fori_loop(0, 36, other_squares, 0)
    sum_in = jnp.sum(squares[0], axis=0, keepdims=True)
    sum_out = jnp.sum(squares[1], axis=0, keepdims=True)
    scale_in[...] = scale_in[...] / jnp.sqrt(sum_in / HD + 1e-06)
    scale_out[...] = scale_out[...] / jnp.sqrt(sum_out / FH + 1e-06)

    @pl.when(z == 0)
    def _():
        first.wait()

    after = (lax.rem(z + 1, NZ), x, y, c)

    def piece(g, carry):
        here = pl.ds(pl.multiple_of(g * PIECE, PIECE), PIECE)

        @pl.when(z > 0)
        def _():
            arrived(rows_in.at[here], z_s.at[g], z_r.at[g], after)

        rows32 = rows_in[here, :].astype(F32)
        scale = lax.rsqrt(jnp.mean(rows32 * rows32, axis=-1, keepdims=True) + 1e-06)
        normed = (rows32 * scale * gains[...]).astype(BF)
        pre = nn(normed, new[0:HD, :]) * scale_in[...]
        gate = pre[:, :FH]
        mixed = (gate * jax.nn.sigmoid(gate) * pre[:, FH:]).astype(BF)
        out[here, :] = (rows32 + nn(mixed, new[HD : HD + FH, :]) * scale_out[...]).astype(BF)

        @pl.when(z < NZ - 1)
        def _():
            remote(out.at[here], rows_in.at[here], z_s.at[g], z_r.at[g], after).start()

        return carry

    lax.fori_loop(0, GROUPS, piece, 0)

    for wait in later:
        wait()

    @pl.when(z < NZ - 1)
    def _():
        def left(g, carry):
            here = pl.ds(pl.multiple_of(g * PIECE, PIECE), PIECE)
            remote(out.at[here], rows_in.at[here], z_s.at[g], z_r.at[g], after).wait_send()
            return carry

        lax.fori_loop(0, GROUPS, left, 0)


def per_device(inputs, keys, values, rates, gains, w_in, w_out):
    c_in, c_out, p_f, p_w, p_jt = constants()
    vm = pl.BlockSpec(memory_space=pltpu.VMEM)
    hb = pl.BlockSpec(memory_space=pltpu.HBM)
    V = pltpu.VMEM
    D = pltpu.SemaphoreType.DMA
    scratch = [
        V((6, 2, HD), BF), V((12, FH), BF), V((1, ROWS), F32), V((1, HD), F32),
        V((48, 64), BF), V((48, 64), BF), V((FH, FH), BF),
        V((ROWS, HD), BF), V((ROWS, HD), BF), V((HD, HD), BF), V((HD, HD), BF), V((ROWS, HD), BF), V((16, HD), F32),
        V((NY, 16, HD), BF), V((NX, 16, FH), BF), V((16, 48, HD), BF), V((16, 48, FH), BF),
        V((HD, ROWS), BF), V((HD, ROWS), BF), V((HD, ROWS), BF), V((FH, ROWS), F32), V((2, FH, ROWS), BF),
        V((FH, ROWS), BF),
        V((576, HD), BF), V((576, HD), BF), V((576, HD), F32), V((NX, 7, 16, HD), BF), V((NX, 7, 16, HD), BF),
        V((NY, 16, HD), BF), V((NY, 16, HD), BF), V((NY, 16, HD), BF), V((NY, 16, HD), BF),
        V((16, HD), BF), V((NX, 16, HD), BF), V((16, HD), F32), V((16, HD), F32), V((16, HD), F32),
        V((16, HD), F32), V((16, HD), F32),
        V((HD + FH, HD), BF), V((2, 16, HD), F32),
        D((12,)),
        D((NY,)), D((NY,)), D((NX,)), D((NX,)), D((2, NX)), D((2, NX)), D((NY,)), D((NY,)),
        D((2, NX)), D((2, NX)), D((NY,)), D((NY,)),
        D((5,)), D((5,)), D((NX, NY)), D((NX, NY)), D((NY,)), D((NY,)), D((NY,)), D((NY,)), D((NX,)), D((NX,)),
        D((NY,)), D((NY,)), D((NY,)), D((NY,)), D((NX, NY)), D((NX, NY)), D((36,)), D((36,)),
        D((GROUPS,)), D((GROUPS,)),
    ]
    result = pl.pallas_call(
        kernel,
        out_shape=jax.ShapeDtypeStruct((ROWS, HD), BF),
        in_specs=[hb] * 12,
        out_specs=vm,
        scratch_shapes=scratch,
        compiler_params=pltpu.CompilerParams(
            collective_id=0, has_side_effects=True, vmem_limit_bytes=63 * 2**20
        ),
        cost_estimate=pl.CostEstimate(flops=1500000000, bytes_accessed=6000000, transcendentals=400000),
    )(w_in, w_out, rates, gains, c_in, c_out, p_f, keys, values, inputs, p_w, p_jt)
    return result[None]


def solution(mesh):
    split = Mesh(
        mesh.devices.reshape(mesh.shape["segment"], NX, NY, NC), ("segment", "tok_0", "tok_1", "tok_2")
    )
    in_specs = (
        P(TOK, None),
        P("segment", TOK, None),
        P("segment", TOK, None),
        P("segment", TOK),
        P("segment", None),
        P("segment", TOK, None, None),
        P("segment", TOK, None),
    )
    return jax.shard_map(
        per_device, mesh=split, in_specs=in_specs, out_specs=P("segment", TOK, None), check_vma=False
    )
```

```python
import functools

import jax
import jax.numpy as jnp
import numpy as np
from jax import lax
from jax.experimental import pallas as pl
from jax.experimental.pallas import tpu as pltpu
from jax.sharding import Mesh
from jax.sharding import PartitionSpec as P

NX, NY, NC, NZ = 4, 8, 2, 8
TOK = ("tok_0", "tok_1", "tok_2")
MESH = pl.DeviceIdType.MESH
F32 = jnp.float32
BF = jnp.bfloat16
HD, FH, ROWS = 768, 384, 256
PIECE = 16
GROUPS = ROWS // PIECE


def constants():
    c_in = np.zeros((48, 64), np.float32)
    for half in range(2):
        for y in range(4):
            for r in range(6):
                c_in[half * 24 + y * 6 + r, y * 16 + r * 2 + half] = 1
    c_out = np.zeros((48, 64), np.float32)
    for x in range(NX):
        for r in range(12):
            c_out[x * 12 + r, x * 16 + r] = 1
    p_f = np.zeros((FH, FH), np.float32)
    for c in range(NC):
        for x in range(NX):
            for y in range(NY):
                for r in range(6):
                    p_f[((x * NY + y) * NC + c) * 6 + r, (c * NX + x) * 48 + y * 6 + r] = 1
    p_w = np.zeros((HD, HD), np.float32)
    for b in range(16):
        for half in range(2):
            for r in range(24):
                p_w[b * 48 + half * 24 + r, half * FH + b * 24 + r] = 1
    p_jt = np.zeros((HD, HD), np.float32)
    for c in range(NC):
        for x in range(NX):
            for y in range(NY):
                for r in range(12):
                    p_jt[(c * NY + y) * 48 + x * 12 + r, ((x * NY + y) * NC + c) * 12 + r] = 1
    return [jnp.asarray(a, BF) for a in (c_in, c_out, p_f, p_w, p_jt)]


def nt(a, b):
    return lax.dot_general(a, b, (((1,), (1,)), ((), ())), preferred_element_type=F32)


def nn(a, b):
    return lax.dot_general(a, b, (((1,), (0,)), ((), ())), preferred_element_type=F32)


def tn(a, b):
    return lax.dot_general(a, b, (((0,), (0,)), ((), ())), preferred_element_type=F32)


def parts(a):
    high = a.astype(BF)
    return high, (a - high.astype(F32)).astype(BF)


def row_squares(w):
    high, low = parts(w.astype(F32) * w.astype(F32))
    ones = jnp.ones((16, w.shape[1]), BF)
    return nt(ones, high) + nt(ones, low)


def moved_by(a, matrix):
    high, low = parts(a)
    return nn(high, matrix) + nn(low, matrix)


NEAR = (1, 7, 2, 6, 3, 5, 4)
FAR = (4, 3, 5, 2, 6, 1, 7)
STEPS = (4, 3, 5, 2, 6, 1, 7, 0)


def kernel(
    win_h, wout_h, rates_h, gains_h, cin_h, cout_h, pf_h, keys_h, vals_h, inputs_h, pw_h, pjt_h,
    out,
    win_own, wout_own, rates, gains, c_in, c_out, p_f, keys, vals, p_w, pjt, rows_in, pad32,
    winpad, woutpad, win, wout,
    keys_t, target_t, targetp_t, dact_t, dhid_t, act_t,
    gs, gr, half, hx_s, hx_r, hy_s, hy_r, ky_s, ky_r, kx_s, kx_r, own_sum, base_x, base_y, scale_in, scale_out,
    new, squares,
    lsem, ya_s, ya_r, xa_s, xa_r, xb_s, xb_r, yb_s, yb_r, cb_s, cb_r, cc_s, cc_r,
    rc_s, rc_r, rx_s, rx_r, ry_s, ry_r, rky_s, rky_r, rkx_s, rkx_r,
    n1_s, n1_r, m2_s, m2_r, n2_s, n2_r, n3_s, n3_r,
    z_s, z_r,
):
    z = lax.axis_index("segment")
    x = lax.axis_index("tok_0")
    y = lax.axis_index("tok_1")
    c = lax.axis_index("tok_2")
    oc = 1 - c

    def ypeer(d):
        return lax.rem(y + d, NY)

    def xpeer(d):
        return lax.rem(x + d, NX)

    def at_y(d):
        return (z, x, ypeer(d), c)

    def at_x(d):
        return (z, xpeer(d), y, c)

    sibling = (z, x, y, oc)
    later = []

    def remote(src, dst, ss, rs, dev):
        return pltpu.make_async_remote_copy(
            src_ref=src, dst_ref=dst, send_sem=ss, recv_sem=rs, device_id=dev, device_id_type=MESH
        )

    def send(src, dst, ss, rs, dev):
        cp = remote(src, dst, ss, rs, dev)
        cp.start()
        later.append(cp.wait_send)

    def send_if(cond, copies, before=None):
        @pl.when(cond)
        def _():
            if before is not None:
                before()
            for cp in copies:
                cp.start()

        @later.append
        @functools.partial(functools.partial, pl.when(cond))
        def _():
            for cp in copies:
                cp.wait_send()

    def finish():
        for wait in later:
            wait()

    def arrived(dst, ss, rs, dev):
        remote(dst, dst, ss, rs, dev).wait_recv()

    pairs = (
        (win_h.at[0], win_own), (wout_h.at[0], wout_own), (pf_h, p_f), (vals_h.at[0], vals), (rates_h, rates),
        (pjt_h, pjt), (cin_h, c_in), (cout_h, c_out), (keys_h.at[0], keys), (pw_h, p_w), (gains_h, gains),
    )
    local = [pltpu.make_async_copy(s, d, lsem.at[i]) for i, (s, d) in enumerate(pairs)]
    for cp in local[:3]:
        cp.start()
    first = pltpu.make_async_copy(inputs_h, rows_in, lsem.at[len(pairs)])

    bar = pltpu.get_barrier_semaphore()
    for d in range(1, NY):
        pl.semaphore_signal(bar, inc=1, device_id=at_y(d), device_id_type=MESH)
    for d in range(1, NX):
        pl.semaphore_signal(bar, inc=1, device_id=at_x(d), device_id_type=MESH)
    pl.semaphore_signal(bar, inc=1, device_id=sibling, device_id_type=MESH)
    for d in (1, NZ - 1):
        pl.semaphore_signal(bar, inc=1, device_id=(lax.rem(z + d, NZ), x, y, c), device_id_type=MESH)
    pad32[...] = jnp.zeros_like(pad32)
    local[0].wait()
    for r in range(6):
        pad32[2 * r : 2 * r + 2, :] = win_own[r].astype(F32)
    winpad[y] = pad32[...].astype(BF)
    pl.semaphore_wait(bar, NY - 1 + NX - 1 + 1 + 2)

    group = y // 4
    place = y - group * 4

    def in_group(g, d):
        return g * 4 + lax.rem(place + d, 4)

    for g, ds in ((group, (2, 1, 3)), (1 - group, (0, 2, 1, 3))):
        for d in ds:
            to = in_group(g, d)
            send(winpad.at[y], winpad.at[y], ya_s.at[to], ya_r.at[y], (z, x, to, c))
    local[1].wait()
    pad32[0:12, 0:FH] = wout_own[...].astype(F32)
    local[2].wait()
    woutpad[x] = nn(pad32[:, 0:FH].astype(BF), p_f[...]).astype(BF)
    for d in range(1, NX):
        send(woutpad.at[x], woutpad.at[x], xa_s.at[d], xa_r.at[d], at_x(d))
    for cp in local[3:]:
        cp.start()

    @pl.when(z == 0)
    def _():
        first.start()

    for cp in local[3:]:
        cp.wait()
    for d in range(1, NX):
        arrived(woutpad.at[xpeer(NX - d)], xa_s.at[d], xa_r.at[d], at_x(d))
    mine_o = c * NY + y
    wout[mine_o] = nn(c_out[...], woutpad[...].reshape(64, FH)).astype(BF)
    for d in FAR:
        send(wout.at[mine_o], wout.at[mine_o], yb_s.at[d], yb_r.at[d], at_y(d))
    send(wout.at[mine_o], wout.at[mine_o], cc_s.at[0], cc_r.at[0], sibling)
    target_t[...] = (vals[...].astype(F32).T * rates[...]).astype(BF)
    for n, (g, ds) in enumerate(((group, (1, 3, 2)), (1 - group, (0, 1, 3, 2)))):
        for d in ds:
            src = in_group(g, d)
            arrived(winpad.at[src], ya_s.at[src], ya_r.at[src], (z, x, src, c))
        mine_i = (c * NX + x) * 2 + g
        win[mine_i] = nn(c_in[...], winpad[pl.ds(g * 4, 4)].reshape(64, HD)).astype(BF)
        for d in (2, 1, 3):
            send(win.at[mine_i], win.at[mine_i], xb_s.at[n, d], xb_r.at[n, d], at_x(d))
        send(win.at[mine_i], win.at[mine_i], cb_s.at[n, 0], cb_r.at[n, 0], sibling)
        if n == 0:
            targetp_t[...] = nn(pjt[...], target_t[...]).astype(BF)
    keys_t[...] = keys[...].astype(F32).T.astype(BF)

    def win_slot(core, d, n):
        return win.at[(core * NX + xpeer(NX - d)) * 2 + (group if n == 0 else 1 - group)]

    for d in NEAR:
        slot = wout.at[c * NY + ypeer(NY - d)]
        arrived(slot, yb_s.at[d], yb_r.at[d], at_y(d))
        send(slot, slot, cc_s.at[d], cc_r.at[d], sibling)
    def x_arrivals(n):
        for d in (1, 3, 2):
            slot = win_slot(c, d, n)
            arrived(slot, xb_s.at[n, d], xb_r.at[n, d], at_x(d))
            send(slot, slot, cb_s.at[n, d], cb_r.at[n, d], sibling)

    x_arrivals(0)
    for d in range(NY):
        arrived(wout.at[oc * NY + ypeer(NY - d)], cc_s.at[d], cc_r.at[d], sibling)
    dact_t[...] = tn(wout[...].reshape(HD, FH), targetp_t[...])
    x_arrivals(1)

    def block(b, carry):
        hidden = nt(win[pl.ds(b * 2, 2)].reshape(96, HD), keys[...]).reshape(2, 2, 24, ROWS)
        gate = hidden[:, 0].reshape(48, ROWS)
        up = hidden[:, 1].reshape(48, ROWS)
        sig = jax.nn.sigmoid(gate)
        silu = gate * sig
        here = pl.ds(pl.multiple_of(b * 48, 16), 48)
        act_t[here, :] = (silu * up).astype(BF)
        da = dact_t[here, :]
        dhid_t[0, here, :] = (da * up * (sig * (1.0 + gate * (1.0 - sig)))).astype(BF)
        dhid_t[1, here, :] = (da * silu).astype(BF)
        return carry

    lax.fori_loop(c * NX, c * NX + NX, block, 0)
    for n in range(2):
        for d in range(NX):
            arrived(win_slot(oc, d, n), cb_s.at[n, d], cb_r.at[n, d], sibling)
    lax.fori_loop(oc * NX, oc * NX + NX, block, 0)

    def out_part(core):
        return nt(act_t[pl.ds(pl.multiple_of(core * 192, 64), 192), :], target_t[...])

    def in_part(core):
        return nt(keys_t[pl.ds(pl.multiple_of(core * FH, FH), FH), :], dhid_t[...].reshape(HD, ROWS))

    def x_rows(d):
        return pl.ds(pl.multiple_of(xpeer(d) * 112, 16), 112)

    y_part = pl.ds(448, 128)
    gs[384:576, :] = out_part(oc).astype(BF)
    send(gs.at[y_part], gr.at[y_part], rc_s.at[4], rc_r.at[4], sibling)
    gs[0:384, :] = in_part(oc).astype(BF)
    for d in (2, 1, 3, 0):
        send(gs.at[x_rows(d)], gr.at[x_rows(d)], rc_s.at[d], rc_r.at[d], sibling)
    half[384:576, :] = out_part(c)
    half[0:384, :] = in_part(c)

    arrived(gr.at[y_part], rc_s.at[4], rc_r.at[4], sibling)
    for k in range(8):
        here = pl.ds(448 + k * 16, 16)
        total = half[here, :] + gr[here, :].astype(F32)
        half[here, :] = total
        hy_s[k] = total.astype(BF)
    for d in FAR:
        send(hy_s.at[ypeer(d)], hy_r.at[y], ry_s.at[d], ry_r.at[d], at_y(d))
    for d in (2, 1, 3, 0):
        arrived(gr.at[x_rows(d)], rc_s.at[d], rc_r.at[d], sibling)
        total = half[x_rows(d), :] + gr[x_rows(d), :].astype(F32)
        if d:
            hx_s[xpeer(d)] = total.reshape(7, 16, HD).astype(BF)
        else:
            half[x_rows(0), :] = total
    for r in STEPS:
        i = ypeer(r)
        send_if(i < 7, [
            remote(hx_s.at[xpeer(d), i], hx_r.at[x, i], rx_s.at[d, i], rx_r.at[d, i], at_x(d)) for d in (2, 1, 3)
        ])

    def row_of(core, k):
        return pl.multiple_of(k * 16 + core * 384 + lax.div(k * 11, 256) * (384 - core * 192), 16)

    lane_in = lax.broadcasted_iota(jnp.int32, (16, HD), 1) - lax.broadcasted_iota(jnp.int32, (16, HD), 0)
    lane_out = lax.broadcasted_iota(jnp.int32, (16, FH), 1) - lax.broadcasted_iota(jnp.int32, (16, FH), 0)

    def base_block(k, ref):
        @pl.when(k < 24)
        def _():
            pick = jnp.where(lane_in == row_of(c, k), 1.0, 0.0).astype(BF)
            ref[...] = nn(nt(pick, win[...].reshape(HD, HD)).astype(BF), p_w[...])

        @pl.when(k >= 24)
        def _():
            pick = jnp.where(lane_out == row_of(c, k) - HD, 1.0, 0.0).astype(BF)
            ref[...] = nn(nt(pick, wout[...].reshape(HD, FH)).astype(BF), pjt[...])

    mine_x = x * 7 + jnp.minimum(y, 6)
    mine_y = 28 + y
    base_block(mine_x, base_x)
    base_block(mine_y, base_y)

    def reduce_step(r):
        i = ypeer(r)

        def reduced():
            total = half[pl.ds(pl.multiple_of(x * 112 + i * 16, 16), 16), :]
            for d in (1, 3, 2):
                src = xpeer(NX - d)
                arrived(hx_r.at[src, i], rx_s.at[d, i], rx_r.at[d, i], at_x(d))
                total = total + hx_r[src, i].astype(F32)
            if r:
                ky_s[i] = total.astype(BF)
            else:
                own_sum[...] = total

        if r:
            send_if(i < 7, [remote(ky_s.at[i], ky_r.at[y], rky_s.at[r], rky_r.at[r], at_y(r))], reduced)
        else:
            pl.when(i < 7)(reduced)

    for r in STEPS[:4]:
        reduce_step(r)
    total = half[pl.ds(pl.multiple_of(448 + y * 16, 16), 16), :]
    for d in NEAR:
        src = ypeer(NY - d)
        arrived(hy_r.at[src], ry_s.at[d], ry_r.at[d], at_y(d))
        total = total + hy_r[src].astype(F32)
    kx_s[...] = total.astype(BF)
    for d in (2, 1, 3):
        send(kx_s, kx_r.at[x], rkx_s.at[d], rkx_r.at[d], at_x(d))
    base_y[...] = base_y[...] + total
    for r in STEPS[4:]:
        reduce_step(r)

    scale_in[...] = jnp.sqrt(moved_by(row_squares(win[...].reshape(HD, HD)), p_w[...]) / HD + 1e-06)
    scale_out[...] = jnp.sqrt(moved_by(row_squares(wout[...].reshape(HD, FH)), pjt[...]) / FH + 1e-06)

    def new_block(core, k):
        return new.at[pl.ds(row_of(core, k), 16)]

    moved = base_y[...]
    for d in (1, 3, 2):
        src = xpeer(NX - d)
        arrived(kx_r.at[src], rkx_s.at[d], rkx_r.at[d], at_x(d))
        moved = moved + kx_r[src].astype(F32)
    mine = new_block(c, mine_y)
    mine[...] = moved.astype(BF)

    mine_first = mine
    mine = new_block(c, mine_x)

    def moved_first():
        moved = base_x[...] + own_sum[...]
        for d in NEAR:
            src = ypeer(NY - d)
            arrived(ky_r.at[src], rky_s.at[d], rky_r.at[d], at_y(d))
            moved = moved + ky_r[src].astype(F32)
        mine[...] = moved.astype(BF)

    def spread(k, i):
        here = new_block(c, k)
        copies = [remote(here, here, n2_s.at[d, i], n2_r.at[d, i], at_x(d)) for d in (2, 1, 3)]
        return copies + [remote(here, here, n3_s.at[k], n3_r.at[k], sibling)]

    send_if(
        y < 7,
        [remote(mine, mine, n1_s.at[d], n1_r.at[d], at_y(d)) for d in FAR] + spread(mine_x, jnp.minimum(y, 6)),
        moved_first,
    )
    for d in FAR:
        send(mine_first, mine_first, m2_s.at[d], m2_r.at[d], at_y(d))
    send(mine_first, mine_first, n3_s.at[mine_y], n3_r.at[mine_y], sibling)
    for d in NEAR:
        src = ypeer(NY - d)
        k = x * 7 + src
        send_if(
            src < 7, spread(k, src), functools.partial(arrived, new_block(c, k), n1_s.at[d], n1_r.at[d], at_y(d))
        )
    for d in NEAR:
        k = 28 + ypeer(NY - d)
        here = new_block(c, k)
        arrived(here, m2_s.at[d], m2_r.at[d], at_y(d))
        send(here, here, n3_s.at[k], n3_r.at[k], sibling)
    for r in (0,) + NEAR:
        i = ypeer(NY - r)
        blocks = [(d, xpeer(NX - d) * 7 + i) for d in (1, 3, 2)]
        waits = [remote(new_block(c, k), new_block(c, k), n2_s.at[d, i], n2_r.at[d, i], at_x(d)) for d, k in blocks]
        copies = [remote(new_block(c, k), new_block(c, k), n3_s.at[k], n3_r.at[k], sibling) for d, k in blocks]

        def x_arrived(waits=waits):
            for cp in waits:
                cp.wait_recv()

        send_if(i < 7, copies, x_arrived)

    def add_squares(core, waits):
        def step(k, total):
            if waits:
                arrived(new_block(core, k), n3_s.at[k], n3_r.at[k], sibling)
            block = new_block(core, k)[...].astype(F32)
            return total + block * block

        for kind, (start, stop) in enumerate(((0, 24), (24, 36))):
            squares[kind] = lax.fori_loop(start, stop, step, squares[kind] if waits else jnp.zeros((16, HD), F32))

    add_squares(c, False)
    add_squares(oc, True)
    sum_in = jnp.sum(squares[0], axis=0, keepdims=True)
    sum_out = jnp.sum(squares[1], axis=0, keepdims=True)
    scale_in[...] = scale_in[...] / jnp.sqrt(sum_in / HD + 1e-06)
    scale_out[...] = scale_out[...] / jnp.sqrt(sum_out / FH + 1e-06)

    @pl.when(z == 0)
    def _():
        first.wait()

    after = (lax.rem(z + 1, NZ), x, y, c)
    pl.when(z >= NZ // 2)(finish)

    def piece(g, carry):
        here = pl.ds(pl.multiple_of(g * PIECE, PIECE), PIECE)

        @pl.when(z > 0)
        def _():
            arrived(rows_in.at[here], z_s.at[g], z_r.at[g], after)

        rows32 = rows_in[here, :].astype(F32)
        scale = lax.rsqrt(jnp.mean(rows32 * rows32, axis=-1, keepdims=True) + 1e-06)
        normed = (rows32 * scale * gains[...]).astype(BF)
        pre = nn(normed, new[0:HD, :]) * scale_in[...]
        gate = pre[:, :FH]
        mixed = (gate * jax.nn.sigmoid(gate) * pre[:, FH:]).astype(BF)
        out[here, :] = (rows32 + nn(mixed, new[HD : HD + FH, :]) * scale_out[...]).astype(BF)

        @pl.when(z < NZ - 1)
        def _():
            remote(out.at[here], rows_in.at[here], z_s.at[g], z_r.at[g], after).start()

        return carry

    lax.fori_loop(0, GROUPS, piece, 0)

    pl.when(z < NZ // 2)(finish)

    @pl.when(z < NZ - 1)
    def _():
        def left(g, carry):
            here = pl.ds(pl.multiple_of(g * PIECE, PIECE), PIECE)
            remote(out.at[here], rows_in.at[here], z_s.at[g], z_r.at[g], after).wait_send()
            return carry

        lax.fori_loop(0, GROUPS, left, 0)


def per_device(inputs, keys, values, rates, gains, w_in, w_out):
    c_in, c_out, p_f, p_w, p_jt = constants()
    vm = pl.BlockSpec(memory_space=pltpu.VMEM)
    hb = pl.BlockSpec(memory_space=pltpu.HBM)
    V = pltpu.VMEM
    D = pltpu.SemaphoreType.DMA
    scratch = [
        V((6, 2, HD), BF), V((12, FH), BF), V((1, ROWS), F32), V((1, HD), F32),
        V((48, 64), BF), V((48, 64), BF), V((FH, FH), BF),
        V((ROWS, HD), BF), V((ROWS, HD), BF), V((HD, HD), BF), V((HD, HD), BF), V((ROWS, HD), BF), V((16, HD), F32),
        V((NY, 16, HD), BF), V((NX, 16, FH), BF), V((16, 48, HD), BF), V((16, 48, FH), BF),
        V((HD, ROWS), BF), V((HD, ROWS), BF), V((HD, ROWS), BF), V((FH, ROWS), F32), V((2, FH, ROWS), BF),
        V((FH, ROWS), BF),
        V((576, HD), BF), V((576, HD), BF), V((576, HD), F32), V((NX, 7, 16, HD), BF), V((NX, 7, 16, HD), BF),
        V((NY, 16, HD), BF), V((NY, 16, HD), BF), V((NY, 16, HD), BF), V((NY, 16, HD), BF),
        V((16, HD), BF), V((NX, 16, HD), BF), V((16, HD), F32), V((16, HD), F32), V((16, HD), F32),
        V((16, HD), F32), V((16, HD), F32),
        V((HD + FH, HD), BF), V((2, 16, HD), F32),
        D((12,)),
        D((NY,)), D((NY,)), D((NX,)), D((NX,)), D((2, NX)), D((2, NX)), D((NY,)), D((NY,)),
        D((2, NX)), D((2, NX)), D((NY,)), D((NY,)),
        D((5,)), D((5,)), D((NX, NY)), D((NX, NY)), D((NY,)), D((NY,)), D((NY,)), D((NY,)), D((NX,)), D((NX,)),
        D((NY,)), D((NY,)), D((NY,)), D((NY,)), D((NX, NY)), D((NX, NY)), D((36,)), D((36,)),
        D((GROUPS,)), D((GROUPS,)),
    ]
    result = pl.pallas_call(
        kernel,
        out_shape=jax.ShapeDtypeStruct((ROWS, HD), BF),
        in_specs=[hb] * 12,
        out_specs=vm,
        scratch_shapes=scratch,
        compiler_params=pltpu.CompilerParams(
            collective_id=0, has_side_effects=True, vmem_limit_bytes=63 * 2**20
        ),
        cost_estimate=pl.CostEstimate(flops=1500000000, bytes_accessed=6000000, transcendentals=400000),
    )(w_in, w_out, rates, gains, c_in, c_out, p_f, keys, values, inputs, p_w, p_jt)
    return result[None]


def solution(mesh):
    split = Mesh(
        mesh.devices.reshape(mesh.shape["segment"], NX, NY, NC), ("segment", "tok_0", "tok_1", "tok_2")
    )
    in_specs = (
        P(TOK, None),
        P("segment", TOK, None),
        P("segment", TOK, None),
        P("segment", TOK),
        P("segment", None),
        P("segment", TOK, None, None),
        P("segment", TOK, None),
    )
    return jax.shard_map(
        per_device, mesh=split, in_specs=in_specs, out_specs=P("segment", TOK, None), check_vma=False
    )
```

```python
import functools

import jax
import jax.numpy as jnp
import numpy as np
from jax import lax
from jax.experimental import pallas as pl
from jax.experimental.pallas import tpu as pltpu
from jax.sharding import Mesh
from jax.sharding import PartitionSpec as P

NX, NY, NC, NZ = 4, 8, 2, 8
TOK = ("tok_0", "tok_1", "tok_2")
MESH = pl.DeviceIdType.MESH
F32 = jnp.float32
BF = jnp.bfloat16
HD, FH, ROWS = 768, 384, 256
PIECE = 16
GROUPS = ROWS // PIECE


def constants():
    c_in = np.zeros((48, 64), np.float32)
    for half in range(2):
        for y in range(4):
            for r in range(6):
                c_in[half * 24 + y * 6 + r, y * 16 + r * 2 + half] = 1
    c_out = np.zeros((48, 64), np.float32)
    for x in range(NX):
        for r in range(12):
            c_out[x * 12 + r, x * 16 + r] = 1
    p_f = np.zeros((FH, FH), np.float32)
    for c in range(NC):
        for x in range(NX):
            for y in range(NY):
                for r in range(6):
                    p_f[((x * NY + y) * NC + c) * 6 + r, (c * NX + x) * 48 + y * 6 + r] = 1
    p_w = np.zeros((HD, HD), np.float32)
    for b in range(16):
        for half in range(2):
            for r in range(24):
                p_w[b * 48 + half * 24 + r, half * FH + b * 24 + r] = 1
    p_jt = np.zeros((HD, HD), np.float32)
    for c in range(NC):
        for x in range(NX):
            for y in range(NY):
                for r in range(12):
                    p_jt[(c * NY + y) * 48 + x * 12 + r, ((x * NY + y) * NC + c) * 12 + r] = 1
    return [jnp.asarray(a, BF) for a in (c_in, c_out, p_f, p_w, p_jt)]


def nt(a, b):
    return lax.dot_general(a, b, (((1,), (1,)), ((), ())), preferred_element_type=F32)


def nn(a, b):
    return lax.dot_general(a, b, (((1,), (0,)), ((), ())), preferred_element_type=F32)


def tn(a, b):
    return lax.dot_general(a, b, (((0,), (0,)), ((), ())), preferred_element_type=F32)


def parts(a):
    high = a.astype(BF)
    return high, (a - high.astype(F32)).astype(BF)


def row_squares(w):
    high, low = parts(w.astype(F32) * w.astype(F32))
    ones = jnp.ones((16, w.shape[1]), BF)
    return nt(ones, high) + nt(ones, low)


def moved_by(a, matrix):
    high, low = parts(a)
    return nn(high, matrix) + nn(low, matrix)


NEAR = (1, 7, 2, 6, 3, 5, 4)
FAR = (4, 3, 5, 2, 6, 1, 7)
STEPS = (4, 3, 5, 2, 6, 1, 7, 0)


def kernel(
    win_h, wout_h, rates_h, gains_h, cin_h, cout_h, pf_h, keys_h, vals_h, inputs_h, pw_h, pjt_h,
    out,
    win_own, wout_own, rates, gains, c_in, c_out, p_f, keys, vals, p_w, pjt, rows_in, pad32,
    winpad, woutpad, win, wout,
    keys_t, target_t, targetp_t, dact_t, dhid_t, act_t,
    gs, gr, half, hx_s, hx_r, hy_s, hy_r, ky_s, ky_r, kx_s, kx_r, own_sum, base_x, base_y, scale_in, scale_out,
    new, squares,
    lsem, ya_s, ya_r, xa_s, xa_r, xb_s, xb_r, yb_s, yb_r, cb_s, cb_r, cc_s, cc_r,
    rc_s, rc_r, rx_s, rx_r, ry_s, ry_r, rky_s, rky_r, rkx_s, rkx_r,
    n1_s, n1_r, m2_s, m2_r, n2_s, n2_r, n3_s, n3_r,
    z_s, z_r,
):
    z = lax.axis_index("segment")
    x = lax.axis_index("tok_0")
    y = lax.axis_index("tok_1")
    c = lax.axis_index("tok_2")
    oc = 1 - c

    def ypeer(d):
        return lax.rem(y + d, NY)

    def xpeer(d):
        return lax.rem(x + d, NX)

    def at_y(d):
        return (z, x, ypeer(d), c)

    def at_x(d):
        return (z, xpeer(d), y, c)

    sibling = (z, x, y, oc)
    later = []

    def remote(src, dst, ss, rs, dev):
        return pltpu.make_async_remote_copy(
            src_ref=src, dst_ref=dst, send_sem=ss, recv_sem=rs, device_id=dev, device_id_type=MESH
        )

    def send(src, dst, ss, rs, dev):
        cp = remote(src, dst, ss, rs, dev)
        cp.start()
        later.append(cp.wait_send)

    def send_if(cond, copies, before=None):
        @pl.when(cond)
        def _():
            if before is not None:
                before()
            for cp in copies:
                cp.start()

        @later.append
        @functools.partial(functools.partial, pl.when(cond))
        def _():
            for cp in copies:
                cp.wait_send()

    def finish():
        for wait in later:
            wait()

    def arrived(dst, ss, rs, dev):
        remote(dst, dst, ss, rs, dev).wait_recv()

    pairs = (
        (win_h.at[0], win_own), (wout_h.at[0], wout_own), (pf_h, p_f), (vals_h.at[0], vals), (rates_h, rates),
        (pjt_h, pjt), (cin_h, c_in), (cout_h, c_out), (keys_h.at[0], keys), (pw_h, p_w), (gains_h, gains),
    )
    local = [pltpu.make_async_copy(s, d, lsem.at[i]) for i, (s, d) in enumerate(pairs)]
    for cp in local[:3]:
        cp.start()
    first = pltpu.make_async_copy(inputs_h, rows_in, lsem.at[len(pairs)])

    bar = pltpu.get_barrier_semaphore()
    for d in range(1, NY):
        pl.semaphore_signal(bar, inc=1, device_id=at_y(d), device_id_type=MESH)
    for d in range(1, NX):
        pl.semaphore_signal(bar, inc=1, device_id=at_x(d), device_id_type=MESH)
    pl.semaphore_signal(bar, inc=1, device_id=sibling, device_id_type=MESH)
    for d in (1, NZ - 1):
        pl.semaphore_signal(bar, inc=1, device_id=(lax.rem(z + d, NZ), x, y, c), device_id_type=MESH)
    pad32[...] = jnp.zeros_like(pad32)
    local[0].wait()
    for r in range(6):
        pad32[2 * r : 2 * r + 2, :] = win_own[r].astype(F32)
    winpad[y] = pad32[...].astype(BF)
    pl.semaphore_wait(bar, NY - 1 + NX - 1 + 1 + 2)

    group = y // 4
    place = y - group * 4

    def in_group(g, d):
        return g * 4 + lax.rem(place + d, 4)

    for g, ds in ((group, (2, 1, 3)), (1 - group, (0, 2, 1, 3))):
        for d in ds:
            to = in_group(g, d)
            send(winpad.at[y], winpad.at[y], ya_s.at[to], ya_r.at[y], (z, x, to, c))
    local[1].wait()
    pad32[0:12, 0:FH] = wout_own[...].astype(F32)
    local[2].wait()
    woutpad[x] = nn(pad32[:, 0:FH].astype(BF), p_f[...]).astype(BF)
    for d in range(1, NX):
        send(woutpad.at[x], woutpad.at[x], xa_s.at[d], xa_r.at[d], at_x(d))
    for cp in local[3:]:
        cp.start()

    @pl.when(z == 0)
    def _():
        first.start()

    for cp in local[3:]:
        cp.wait()
    for d in range(1, NX):
        arrived(woutpad.at[xpeer(NX - d)], xa_s.at[d], xa_r.at[d], at_x(d))
    mine_o = c * NY + y
    wout[mine_o] = nn(c_out[...], woutpad[...].reshape(64, FH)).astype(BF)
    for d in FAR:
        send(wout.at[mine_o], wout.at[mine_o], yb_s.at[d], yb_r.at[d], at_y(d))
    send(wout.at[mine_o], wout.at[mine_o], cc_s.at[0], cc_r.at[0], sibling)
    target_t[...] = (vals[...].astype(F32).T * rates[...]).astype(BF)
    for n, (g, ds) in enumerate(((group, (1, 3, 2)), (1 - group, (0, 1, 3, 2)))):
        for d in ds:
            src = in_group(g, d)
            arrived(winpad.at[src], ya_s.at[src], ya_r.at[src], (z, x, src, c))
        mine_i = (c * NX + x) * 2 + g
        win[mine_i] = nn(c_in[...], winpad[pl.ds(g * 4, 4)].reshape(64, HD)).astype(BF)
        for d in (2, 1, 3):
            send(win.at[mine_i], win.at[mine_i], xb_s.at[n, d], xb_r.at[n, d], at_x(d))
        send(win.at[mine_i], win.at[mine_i], cb_s.at[n, 0], cb_r.at[n, 0], sibling)
        if n == 0:
            targetp_t[...] = nn(pjt[...], target_t[...]).astype(BF)
    keys_t[...] = keys[...].astype(F32).T.astype(BF)

    def win_slot(core, d, n):
        return win.at[(core * NX + xpeer(NX - d)) * 2 + (group if n == 0 else 1 - group)]

    for d in NEAR:
        slot = wout.at[c * NY + ypeer(NY - d)]
        arrived(slot, yb_s.at[d], yb_r.at[d], at_y(d))
        send(slot, slot, cc_s.at[d], cc_r.at[d], sibling)
    def x_arrivals(n):
        for d in (1, 3, 2):
            slot = win_slot(c, d, n)
            arrived(slot, xb_s.at[n, d], xb_r.at[n, d], at_x(d))
            send(slot, slot, cb_s.at[n, d], cb_r.at[n, d], sibling)

    x_arrivals(0)
    for d in range(NY):
        arrived(wout.at[oc * NY + ypeer(NY - d)], cc_s.at[d], cc_r.at[d], sibling)
    dact_t[...] = tn(wout[...].reshape(HD, FH), targetp_t[...])
    x_arrivals(1)

    def block(b, carry):
        hidden = nt(win[pl.ds(b * 2, 2)].reshape(96, HD), keys[...]).reshape(2, 2, 24, ROWS)
        gate = hidden[:, 0].reshape(48, ROWS)
        up = hidden[:, 1].reshape(48, ROWS)
        sig = jax.nn.sigmoid(gate)
        silu = gate * sig
        here = pl.ds(pl.multiple_of(b * 48, 16), 48)
        act_t[here, :] = (silu * up).astype(BF)
        da = dact_t[here, :]
        dhid_t[0, here, :] = (da * up * (sig * (1.0 + gate * (1.0 - sig)))).astype(BF)
        dhid_t[1, here, :] = (da * silu).astype(BF)
        return carry

    lax.fori_loop(c * NX, c * NX + NX, block, 0)
    for n in range(2):
        for d in range(NX):
            arrived(win_slot(oc, d, n), cb_s.at[n, d], cb_r.at[n, d], sibling)
    lax.fori_loop(oc * NX, oc * NX + NX, block, 0)

    def out_part(core):
        return nt(act_t[pl.ds(pl.multiple_of(core * 192, 64), 192), :], target_t[...])

    def in_part(core):
        return nt(keys_t[pl.ds(pl.multiple_of(core * FH, FH), FH), :], dhid_t[...].reshape(HD, ROWS))

    def x_rows(d):
        return pl.ds(pl.multiple_of(xpeer(d) * 112, 16), 112)

    y_part = pl.ds(448, 128)
    gs[384:576, :] = out_part(oc).astype(BF)
    send(gs.at[y_part], gr.at[y_part], rc_s.at[4], rc_r.at[4], sibling)
    gs[0:384, :] = in_part(oc).astype(BF)
    for d in (2, 1, 3, 0):
        send(gs.at[x_rows(d)], gr.at[x_rows(d)], rc_s.at[d], rc_r.at[d], sibling)
    half[384:576, :] = out_part(c)
    half[0:384, :] = in_part(c)

    arrived(gr.at[y_part], rc_s.at[4], rc_r.at[4], sibling)
    for k in range(8):
        here = pl.ds(448 + k * 16, 16)
        total = half[here, :] + gr[here, :].astype(F32)
        half[here, :] = total
        hy_s[k] = total.astype(BF)
    for d in FAR:
        send(hy_s.at[ypeer(d)], hy_r.at[y], ry_s.at[d], ry_r.at[d], at_y(d))
    for d in (2, 1, 3, 0):
        arrived(gr.at[x_rows(d)], rc_s.at[d], rc_r.at[d], sibling)
        total = half[x_rows(d), :] + gr[x_rows(d), :].astype(F32)
        if d:
            hx_s[xpeer(d)] = total.reshape(7, 16, HD).astype(BF)
        else:
            half[x_rows(0), :] = total
    for r in STEPS:
        i = ypeer(r)
        send_if(i < 7, [
            remote(hx_s.at[xpeer(d), i], hx_r.at[x, i], rx_s.at[d, i], rx_r.at[d, i], at_x(d)) for d in (2, 1, 3)
        ])

    def row_of(core, k):
        return pl.multiple_of(k * 16 + core * 384 + lax.div(k * 11, 256) * (384 - core * 192), 16)

    lane_in = lax.broadcasted_iota(jnp.int32, (16, HD), 1) - lax.broadcasted_iota(jnp.int32, (16, HD), 0)
    lane_out = lax.broadcasted_iota(jnp.int32, (16, FH), 1) - lax.broadcasted_iota(jnp.int32, (16, FH), 0)

    def base_block(k, ref):
        @pl.when(k < 24)
        def _():
            pick = jnp.where(lane_in == row_of(c, k), 1.0, 0.0).astype(BF)
            ref[...] = nn(nt(pick, win[...].reshape(HD, HD)).astype(BF), p_w[...])

        @pl.when(k >= 24)
        def _():
            pick = jnp.where(lane_out == row_of(c, k) - HD, 1.0, 0.0).astype(BF)
            ref[...] = nn(nt(pick, wout[...].reshape(HD, FH)).astype(BF), pjt[...])

    mine_x = x * 7 + jnp.minimum(y, 6)
    mine_y = 28 + y
    base_block(mine_x, base_x)
    base_block(mine_y, base_y)

    def reduce_step(r):
        i = ypeer(r)

        def reduced():
            total = half[pl.ds(pl.multiple_of(x * 112 + i * 16, 16), 16), :]
            for d in (1, 3, 2):
                src = xpeer(NX - d)
                arrived(hx_r.at[src, i], rx_s.at[d, i], rx_r.at[d, i], at_x(d))
                total = total + hx_r[src, i].astype(F32)
            if r:
                ky_s[i] = total.astype(BF)
            else:
                own_sum[...] = total

        if r:
            send_if(i < 7, [remote(ky_s.at[i], ky_r.at[y], rky_s.at[r], rky_r.at[r], at_y(r))], reduced)
        else:
            pl.when(i < 7)(reduced)

    for r in STEPS[:4]:
        reduce_step(r)
    total = half[pl.ds(pl.multiple_of(448 + y * 16, 16), 16), :]
    for d in NEAR:
        src = ypeer(NY - d)
        arrived(hy_r.at[src], ry_s.at[d], ry_r.at[d], at_y(d))
        total = total + hy_r[src].astype(F32)
    kx_s[...] = total.astype(BF)
    for d in (2, 1, 3):
        send(kx_s, kx_r.at[x], rkx_s.at[d], rkx_r.at[d], at_x(d))
    base_y[...] = base_y[...] + total
    for r in STEPS[4:]:
        reduce_step(r)

    scale_in[...] = jnp.sqrt(moved_by(row_squares(win[...].reshape(HD, HD)), p_w[...]) / HD + 1e-06)
    scale_out[...] = jnp.sqrt(moved_by(row_squares(wout[...].reshape(HD, FH)), pjt[...]) / FH + 1e-06)

    def new_block(core, k):
        return new.at[pl.ds(row_of(core, k), 16)]

    moved = base_y[...]
    for d in (1, 3, 2):
        src = xpeer(NX - d)
        arrived(kx_r.at[src], rkx_s.at[d], rkx_r.at[d], at_x(d))
        moved = moved + kx_r[src].astype(F32)
    mine = new_block(c, mine_y)
    mine[...] = moved.astype(BF)

    mine_first = mine
    mine = new_block(c, mine_x)

    def moved_first():
        moved = base_x[...] + own_sum[...]
        for d in NEAR:
            src = ypeer(NY - d)
            arrived(ky_r.at[src], rky_s.at[d], rky_r.at[d], at_y(d))
            moved = moved + ky_r[src].astype(F32)
        mine[...] = moved.astype(BF)

    def spread(k, i):
        here = new_block(c, k)
        copies = [remote(here, here, n2_s.at[d, i], n2_r.at[d, i], at_x(d)) for d in (2, 1, 3)]
        return copies + [remote(here, here, n3_s.at[k], n3_r.at[k], sibling)]

    send_if(
        y < 7,
        [remote(mine, mine, n1_s.at[d], n1_r.at[d], at_y(d)) for d in FAR] + spread(mine_x, jnp.minimum(y, 6)),
        moved_first,
    )
    for d in FAR:
        send(mine_first, mine_first, m2_s.at[d], m2_r.at[d], at_y(d))
    send(mine_first, mine_first, n3_s.at[mine_y], n3_r.at[mine_y], sibling)
    for d in NEAR:
        src = ypeer(NY - d)
        k = x * 7 + src
        send_if(
            src < 7, spread(k, src), functools.partial(arrived, new_block(c, k), n1_s.at[d], n1_r.at[d], at_y(d))
        )
    for d in NEAR:
        k = 28 + ypeer(NY - d)
        here = new_block(c, k)
        arrived(here, m2_s.at[d], m2_r.at[d], at_y(d))
        send(here, here, n3_s.at[k], n3_r.at[k], sibling)
    for r in (0,) + NEAR:
        i = ypeer(NY - r)
        blocks = [(d, xpeer(NX - d) * 7 + i) for d in (1, 3, 2)]
        waits = [remote(new_block(c, k), new_block(c, k), n2_s.at[d, i], n2_r.at[d, i], at_x(d)) for d, k in blocks]
        copies = [remote(new_block(c, k), new_block(c, k), n3_s.at[k], n3_r.at[k], sibling) for d, k in blocks]

        def x_arrived(waits=waits):
            for cp in waits:
                cp.wait_recv()

        send_if(i < 7, copies, x_arrived)

    def add_squares(core, waits):
        def step(k, total):
            if waits:
                arrived(new_block(core, k), n3_s.at[k], n3_r.at[k], sibling)
            block = new_block(core, k)[...].astype(F32)
            return total + block * block

        for kind, (start, stop) in enumerate(((0, 24), (24, 36))):
            squares[kind] = lax.fori_loop(start, stop, step, squares[kind] if waits else jnp.zeros((16, HD), F32))

    add_squares(c, False)
    add_squares(oc, True)
    sum_in = jnp.sum(squares[0], axis=0, keepdims=True)
    sum_out = jnp.sum(squares[1], axis=0, keepdims=True)
    scale_in[...] = scale_in[...] / jnp.sqrt(sum_in / HD + 1e-06)
    scale_out[...] = scale_out[...] / jnp.sqrt(sum_out / FH + 1e-06)

    @pl.when(z == 0)
    def _():
        first.wait()

    after = (lax.rem(z + 1, NZ), x, y, c)
    pl.when(z >= NZ // 2)(finish)

    def piece(g, carry):
        here = pl.ds(pl.multiple_of(g * PIECE, PIECE), PIECE)

        @pl.when(z > 0)
        def _():
            arrived(rows_in.at[here], z_s.at[g], z_r.at[g], after)

        rows32 = rows_in[here, :].astype(F32)
        scale = lax.rsqrt(jnp.mean(rows32 * rows32, axis=-1, keepdims=True) + 1e-06)
        pre = nn((rows32 * gains[...]).astype(BF), new[0:HD, :]) * scale * scale_in[...]
        gate = pre[:, :FH]
        mixed = (gate * jax.nn.sigmoid(gate) * pre[:, FH:]).astype(BF)
        out[here, :] = (rows32 + nn(mixed, new[HD : HD + FH, :]) * scale_out[...]).astype(BF)

        @pl.when(z < NZ - 1)
        def _():
            remote(out.at[here], rows_in.at[here], z_s.at[g], z_r.at[g], after).start()

        return carry

    lax.fori_loop(0, GROUPS, piece, 0)

    pl.when(z < NZ // 2)(finish)

    @pl.when(z < NZ - 1)
    def _():
        def left(g, carry):
            here = pl.ds(pl.multiple_of(g * PIECE, PIECE), PIECE)
            remote(out.at[here], rows_in.at[here], z_s.at[g], z_r.at[g], after).wait_send()
            return carry

        lax.fori_loop(0, GROUPS, left, 0)


def per_device(inputs, keys, values, rates, gains, w_in, w_out):
    c_in, c_out, p_f, p_w, p_jt = constants()
    vm = pl.BlockSpec(memory_space=pltpu.VMEM)
    hb = pl.BlockSpec(memory_space=pltpu.HBM)
    V = pltpu.VMEM
    D = pltpu.SemaphoreType.DMA
    scratch = [
        V((6, 2, HD), BF), V((12, FH), BF), V((1, ROWS), F32), V((1, HD), F32),
        V((48, 64), BF), V((48, 64), BF), V((FH, FH), BF),
        V((ROWS, HD), BF), V((ROWS, HD), BF), V((HD, HD), BF), V((HD, HD), BF), V((ROWS, HD), BF), V((16, HD), F32),
        V((NY, 16, HD), BF), V((NX, 16, FH), BF), V((16, 48, HD), BF), V((16, 48, FH), BF),
        V((HD, ROWS), BF), V((HD, ROWS), BF), V((HD, ROWS), BF), V((FH, ROWS), F32), V((2, FH, ROWS), BF),
        V((FH, ROWS), BF),
        V((576, HD), BF), V((576, HD), BF), V((576, HD), F32), V((NX, 7, 16, HD), BF), V((NX, 7, 16, HD), BF),
        V((NY, 16, HD), BF), V((NY, 16, HD), BF), V((NY, 16, HD), BF), V((NY, 16, HD), BF),
        V((16, HD), BF), V((NX, 16, HD), BF), V((16, HD), F32), V((16, HD), F32), V((16, HD), F32),
        V((16, HD), F32), V((16, HD), F32),
        V((HD + FH, HD), BF), V((2, 16, HD), F32),
        D((12,)),
        D((NY,)), D((NY,)), D((NX,)), D((NX,)), D((2, NX)), D((2, NX)), D((NY,)), D((NY,)),
        D((2, NX)), D((2, NX)), D((NY,)), D((NY,)),
        D((5,)), D((5,)), D((NX, NY)), D((NX, NY)), D((NY,)), D((NY,)), D((NY,)), D((NY,)), D((NX,)), D((NX,)),
        D((NY,)), D((NY,)), D((NY,)), D((NY,)), D((NX, NY)), D((NX, NY)), D((36,)), D((36,)),
        D((GROUPS,)), D((GROUPS,)),
    ]
    result = pl.pallas_call(
        kernel,
        out_shape=jax.ShapeDtypeStruct((ROWS, HD), BF),
        in_specs=[hb] * 12,
        out_specs=vm,
        scratch_shapes=scratch,
        compiler_params=pltpu.CompilerParams(
            collective_id=0, has_side_effects=True, vmem_limit_bytes=63 * 2**20
        ),
        cost_estimate=pl.CostEstimate(flops=1500000000, bytes_accessed=6000000, transcendentals=400000),
    )(w_in, w_out, rates, gains, c_in, c_out, p_f, keys, values, inputs, p_w, p_jt)
    return result[None]


def solution(mesh):
    split = Mesh(
        mesh.devices.reshape(mesh.shape["segment"], NX, NY, NC), ("segment", "tok_0", "tok_1", "tok_2")
    )
    in_specs = (
        P(TOK, None),
        P("segment", TOK, None),
        P("segment", TOK, None),
        P("segment", TOK),
        P("segment", None),
        P("segment", TOK, None, None),
        P("segment", TOK, None),
    )
    return jax.shard_map(
        per_device, mesh=split, in_specs=in_specs, out_specs=P("segment", TOK, None), check_vma=False
    )
```

```python
import functools

import jax
import jax.numpy as jnp
import numpy as np
from jax import lax
from jax.experimental import pallas as pl
from jax.experimental.pallas import tpu as pltpu
from jax.sharding import Mesh
from jax.sharding import PartitionSpec as P

NX, NY, NC, NZ = 4, 8, 2, 8
TOK = ("tok_0", "tok_1", "tok_2")
MESH = pl.DeviceIdType.MESH
F32 = jnp.float32
BF = jnp.bfloat16
HD, FH, ROWS = 768, 384, 256
PIECE = 16
GROUPS = ROWS // PIECE


def constants():
    c_in = np.zeros((48, 64), np.float32)
    for half in range(2):
        for y in range(4):
            for r in range(6):
                c_in[half * 24 + y * 6 + r, y * 16 + r * 2 + half] = 1
    c_out = np.zeros((48, 64), np.float32)
    for x in range(NX):
        for r in range(12):
            c_out[x * 12 + r, x * 16 + r] = 1
    p_f = np.zeros((FH, FH), np.float32)
    for c in range(NC):
        for x in range(NX):
            for y in range(NY):
                for r in range(6):
                    p_f[((x * NY + y) * NC + c) * 6 + r, (c * NX + x) * 48 + y * 6 + r] = 1
    p_w = np.zeros((HD, HD), np.float32)
    for b in range(16):
        for half in range(2):
            for r in range(24):
                p_w[b * 48 + half * 24 + r, half * FH + b * 24 + r] = 1
    p_jt = np.zeros((HD, HD), np.float32)
    for c in range(NC):
        for x in range(NX):
            for y in range(NY):
                for r in range(12):
                    p_jt[(c * NY + y) * 48 + x * 12 + r, ((x * NY + y) * NC + c) * 12 + r] = 1
    return [jnp.asarray(a, BF) for a in (c_in, c_out, p_f, p_w, p_jt)]


def nt(a, b):
    return lax.dot_general(a, b, (((1,), (1,)), ((), ())), preferred_element_type=F32)


def nn(a, b):
    return lax.dot_general(a, b, (((1,), (0,)), ((), ())), preferred_element_type=F32)


def tn(a, b):
    return lax.dot_general(a, b, (((0,), (0,)), ((), ())), preferred_element_type=F32)


def parts(a):
    high = a.astype(BF)
    return high, (a - high.astype(F32)).astype(BF)


def row_squares(w):
    squared = w.astype(F32) * w.astype(F32)
    return nt(jnp.ones((16, w.shape[1]), BF), squared.astype(BF))


def moved_by(a, matrix):
    high, low = parts(a)
    return nn(high, matrix) + nn(low, matrix)


NEAR = (1, 7, 2, 6, 3, 5, 4)
FAR = (4, 3, 5, 2, 6, 1, 7)
STEPS = (4, 3, 5, 2, 6, 1, 7, 0)


def kernel(
    win_h, wout_h, rates_h, gains_h, cin_h, cout_h, pf_h, keys_h, vals_h, inputs_h, pw_h, pjt_h,
    out,
    win_own, wout_own, rates, gains, c_in, c_out, p_f, keys, vals, p_w, pjt, rows_in, pad32,
    winpad, woutpad, win, wout,
    keys_t, target_t, targetp_t, dact_t, dhid_t, act_t,
    gs, gr, half, hx_s, hx_r, hy_s, hy_r, ky_s, ky_r, kx_s, kx_r, own_sum, base_x, base_y, scale_in, scale_out,
    new, squares,
    lsem, ya_s, ya_r, xa_s, xa_r, xb_s, xb_r, yb_s, yb_r, cb_s, cb_r, cc_s, cc_r,
    rc_s, rc_r, rx_s, rx_r, ry_s, ry_r, rky_s, rky_r, rkx_s, rkx_r,
    n1_s, n1_r, m2_s, m2_r, n2_s, n2_r, n3_s, n3_r,
    z_s, z_r,
):
    z = lax.axis_index("segment")
    x = lax.axis_index("tok_0")
    y = lax.axis_index("tok_1")
    c = lax.axis_index("tok_2")
    oc = 1 - c

    def ypeer(d):
        return lax.rem(y + d, NY)

    def xpeer(d):
        return lax.rem(x + d, NX)

    def at_y(d):
        return (z, x, ypeer(d), c)

    def at_x(d):
        return (z, xpeer(d), y, c)

    sibling = (z, x, y, oc)
    later = []

    def remote(src, dst, ss, rs, dev):
        return pltpu.make_async_remote_copy(
            src_ref=src, dst_ref=dst, send_sem=ss, recv_sem=rs, device_id=dev, device_id_type=MESH
        )

    def send(src, dst, ss, rs, dev):
        cp = remote(src, dst, ss, rs, dev)
        cp.start()
        later.append(cp.wait_send)

    def send_if(cond, copies, before=None):
        @pl.when(cond)
        def _():
            if before is not None:
                before()
            for cp in copies:
                cp.start()

        @later.append
        @functools.partial(functools.partial, pl.when(cond))
        def _():
            for cp in copies:
                cp.wait_send()

    def finish():
        for wait in later:
            wait()

    def arrived(dst, ss, rs, dev):
        remote(dst, dst, ss, rs, dev).wait_recv()

    pairs = (
        (win_h.at[0], win_own), (wout_h.at[0], wout_own), (pf_h, p_f), (vals_h.at[0], vals), (rates_h, rates),
        (pjt_h, pjt), (cin_h, c_in), (cout_h, c_out), (keys_h.at[0], keys), (pw_h, p_w), (gains_h, gains),
    )
    local = [pltpu.make_async_copy(s, d, lsem.at[i]) for i, (s, d) in enumerate(pairs)]
    for cp in local[:3]:
        cp.start()
    first = pltpu.make_async_copy(inputs_h, rows_in, lsem.at[len(pairs)])

    bar = pltpu.get_barrier_semaphore()
    for d in range(1, NY):
        pl.semaphore_signal(bar, inc=1, device_id=at_y(d), device_id_type=MESH)
    for d in range(1, NX):
        pl.semaphore_signal(bar, inc=1, device_id=at_x(d), device_id_type=MESH)
    pl.semaphore_signal(bar, inc=1, device_id=sibling, device_id_type=MESH)
    for d in (1, NZ - 1):
        pl.semaphore_signal(bar, inc=1, device_id=(lax.rem(z + d, NZ), x, y, c), device_id_type=MESH)
    pad32[...] = jnp.zeros_like(pad32)
    local[0].wait()
    for r in range(6):
        pad32[2 * r : 2 * r + 2, :] = win_own[r].astype(F32)
    winpad[y] = pad32[...].astype(BF)
    pl.semaphore_wait(bar, NY - 1 + NX - 1 + 1 + 2)

    group = y // 4
    place = y - group * 4

    def in_group(g, d):
        return g * 4 + lax.rem(place + d, 4)

    for g, ds in ((group, (2, 1, 3)), (1 - group, (0, 2, 1, 3))):
        for d in ds:
            to = in_group(g, d)
            send(winpad.at[y], winpad.at[y], ya_s.at[to], ya_r.at[y], (z, x, to, c))
    local[1].wait()
    pad32[0:12, 0:FH] = wout_own[...].astype(F32)
    local[2].wait()
    woutpad[x] = nn(pad32[:, 0:FH].astype(BF), p_f[...]).astype(BF)
    for d in range(1, NX):
        send(woutpad.at[x], woutpad.at[x], xa_s.at[d], xa_r.at[d], at_x(d))
    for cp in local[3:]:
        cp.start()

    @pl.when(z == 0)
    def _():
        first.start()

    for cp in local[3:]:
        cp.wait()
    for d in range(1, NX):
        arrived(woutpad.at[xpeer(NX - d)], xa_s.at[d], xa_r.at[d], at_x(d))
    mine_o = c * NY + y
    wout[mine_o] = nn(c_out[...], woutpad[...].reshape(64, FH)).astype(BF)
    for d in FAR:
        send(wout.at[mine_o], wout.at[mine_o], yb_s.at[d], yb_r.at[d], at_y(d))
    send(wout.at[mine_o], wout.at[mine_o], cc_s.at[0], cc_r.at[0], sibling)
    target_t[...] = (vals[...].astype(F32).T * rates[...]).astype(BF)
    for n, (g, ds) in enumerate(((group, (1, 3, 2)), (1 - group, (0, 1, 3, 2)))):
        for d in ds:
            src = in_group(g, d)
            arrived(winpad.at[src], ya_s.at[src], ya_r.at[src], (z, x, src, c))
        mine_i = (c * NX + x) * 2 + g
        win[mine_i] = nn(c_in[...], winpad[pl.ds(g * 4, 4)].reshape(64, HD)).astype(BF)
        for d in (2, 1, 3):
            send(win.at[mine_i], win.at[mine_i], xb_s.at[n, d], xb_r.at[n, d], at_x(d))
        send(win.at[mine_i], win.at[mine_i], cb_s.at[n, 0], cb_r.at[n, 0], sibling)
        if n == 0:
            targetp_t[...] = nn(pjt[...], target_t[...]).astype(BF)
    keys_t[...] = keys[...].astype(F32).T.astype(BF)

    def win_slot(core, d, n):
        return win.at[(core * NX + xpeer(NX - d)) * 2 + (group if n == 0 else 1 - group)]

    for d in NEAR:
        slot = wout.at[c * NY + ypeer(NY - d)]
        arrived(slot, yb_s.at[d], yb_r.at[d], at_y(d))
        send(slot, slot, cc_s.at[d], cc_r.at[d], sibling)
    def x_arrivals(n):
        for d in (1, 3, 2):
            slot = win_slot(c, d, n)
            arrived(slot, xb_s.at[n, d], xb_r.at[n, d], at_x(d))
            send(slot, slot, cb_s.at[n, d], cb_r.at[n, d], sibling)

    x_arrivals(0)
    for d in range(NY):
        arrived(wout.at[oc * NY + ypeer(NY - d)], cc_s.at[d], cc_r.at[d], sibling)
    dact_t[...] = tn(wout[...].reshape(HD, FH), targetp_t[...])
    x_arrivals(1)

    def block(b, carry):
        hidden = nt(win[pl.ds(b * 2, 2)].reshape(96, HD), keys[...]).reshape(2, 2, 24, ROWS)
        gate = hidden[:, 0].reshape(48, ROWS)
        up = hidden[:, 1].reshape(48, ROWS)
        sig = jax.nn.sigmoid(gate)
        silu = gate * sig
        here = pl.ds(pl.multiple_of(b * 48, 16), 48)
        act_t[here, :] = (silu * up).astype(BF)
        da = dact_t[here, :]
        dhid_t[0, here, :] = (da * up * (sig * (1.0 + gate * (1.0 - sig)))).astype(BF)
        dhid_t[1, here, :] = (da * silu).astype(BF)
        return carry

    lax.fori_loop(c * NX, c * NX + NX, block, 0)
    for n in range(2):
        for d in range(NX):
            arrived(win_slot(oc, d, n), cb_s.at[n, d], cb_r.at[n, d], sibling)
    lax.fori_loop(oc * NX, oc * NX + NX, block, 0)

    def out_part(core):
        return nt(act_t[pl.ds(pl.multiple_of(core * 192, 64), 192), :], target_t[...])

    def in_part(core):
        return nt(keys_t[pl.ds(pl.multiple_of(core * FH, FH), FH), :], dhid_t[...].reshape(HD, ROWS))

    def x_rows(d):
        return pl.ds(pl.multiple_of(xpeer(d) * 112, 16), 112)

    y_part = pl.ds(448, 128)
    gs[384:576, :] = out_part(oc).astype(BF)
    send(gs.at[y_part], gr.at[y_part], rc_s.at[4], rc_r.at[4], sibling)
    gs[0:384, :] = in_part(oc).astype(BF)
    for d in (2, 1, 3, 0):
        send(gs.at[x_rows(d)], gr.at[x_rows(d)], rc_s.at[d], rc_r.at[d], sibling)
    half[384:576, :] = out_part(c)
    half[0:384, :] = in_part(c)

    arrived(gr.at[y_part], rc_s.at[4], rc_r.at[4], sibling)
    for k in range(8):
        here = pl.ds(448 + k * 16, 16)
        total = half[here, :] + gr[here, :].astype(F32)
        half[here, :] = total
        hy_s[k] = total.astype(BF)
    for d in FAR:
        send(hy_s.at[ypeer(d)], hy_r.at[y], ry_s.at[d], ry_r.at[d], at_y(d))
    for d in (2, 1, 3, 0):
        arrived(gr.at[x_rows(d)], rc_s.at[d], rc_r.at[d], sibling)
        total = half[x_rows(d), :] + gr[x_rows(d), :].astype(F32)
        if d:
            hx_s[xpeer(d)] = total.reshape(7, 16, HD).astype(BF)
        else:
            half[x_rows(0), :] = total
    for r in STEPS:
        i = ypeer(r)
        send_if(i < 7, [
            remote(hx_s.at[xpeer(d), i], hx_r.at[x, i], rx_s.at[d, i], rx_r.at[d, i], at_x(d)) for d in (2, 1, 3)
        ])

    def row_of(core, k):
        return pl.multiple_of(k * 16 + core * 384 + lax.div(k * 11, 256) * (384 - core * 192), 16)

    lane_in = lax.broadcasted_iota(jnp.int32, (16, HD), 1) - lax.broadcasted_iota(jnp.int32, (16, HD), 0)
    lane_out = lax.broadcasted_iota(jnp.int32, (16, FH), 1) - lax.broadcasted_iota(jnp.int32, (16, FH), 0)

    def base_block(k, ref):
        @pl.when(k < 24)
        def _():
            pick = jnp.where(lane_in == row_of(c, k), 1.0, 0.0).astype(BF)
            ref[...] = nn(nt(pick, win[...].reshape(HD, HD)).astype(BF), p_w[...])

        @pl.when(k >= 24)
        def _():
            pick = jnp.where(lane_out == row_of(c, k) - HD, 1.0, 0.0).astype(BF)
            ref[...] = nn(nt(pick, wout[...].reshape(HD, FH)).astype(BF), pjt[...])

    mine_x = x * 7 + jnp.minimum(y, 6)
    mine_y = 28 + y
    base_block(mine_x, base_x)
    base_block(mine_y, base_y)
    scale_in[...] = jnp.sqrt(moved_by(row_squares(win[...].reshape(HD, HD)), p_w[...]) / HD + 1e-06)

    def reduce_step(r):
        i = ypeer(r)

        def reduced():
            total = half[pl.ds(pl.multiple_of(x * 112 + i * 16, 16), 16), :]
            for d in (1, 3, 2):
                src = xpeer(NX - d)
                arrived(hx_r.at[src, i], rx_s.at[d, i], rx_r.at[d, i], at_x(d))
                total = total + hx_r[src, i].astype(F32)
            if r:
                ky_s[i] = total.astype(BF)
            else:
                own_sum[...] = total

        if r:
            send_if(i < 7, [remote(ky_s.at[i], ky_r.at[y], rky_s.at[r], rky_r.at[r], at_y(r))], reduced)
        else:
            pl.when(i < 7)(reduced)

    for r in STEPS[:4]:
        reduce_step(r)
    total = half[pl.ds(pl.multiple_of(448 + y * 16, 16), 16), :]
    for d in NEAR:
        src = ypeer(NY - d)
        arrived(hy_r.at[src], ry_s.at[d], ry_r.at[d], at_y(d))
        total = total + hy_r[src].astype(F32)
    kx_s[...] = total.astype(BF)
    for d in (2, 1, 3):
        send(kx_s, kx_r.at[x], rkx_s.at[d], rkx_r.at[d], at_x(d))
    base_y[...] = base_y[...] + total
    for r in STEPS[4:]:
        reduce_step(r)

    scale_out[...] = jnp.sqrt(moved_by(row_squares(wout[...].reshape(HD, FH)), pjt[...]) / FH + 1e-06)

    def new_block(core, k):
        return new.at[pl.ds(row_of(core, k), 16)]

    moved = base_y[...]
    for d in (1, 3, 2):
        src = xpeer(NX - d)
        arrived(kx_r.at[src], rkx_s.at[d], rkx_r.at[d], at_x(d))
        moved = moved + kx_r[src].astype(F32)
    mine = new_block(c, mine_y)
    mine[...] = moved.astype(BF)

    mine_first = mine
    mine = new_block(c, mine_x)

    def moved_first():
        moved = base_x[...] + own_sum[...]
        for d in NEAR:
            src = ypeer(NY - d)
            arrived(ky_r.at[src], rky_s.at[d], rky_r.at[d], at_y(d))
            moved = moved + ky_r[src].astype(F32)
        mine[...] = moved.astype(BF)

    def spread(k, i):
        here = new_block(c, k)
        copies = [remote(here, here, n2_s.at[d, i], n2_r.at[d, i], at_x(d)) for d in (2, 1, 3)]
        return copies + [remote(here, here, n3_s.at[k], n3_r.at[k], sibling)]

    send_if(
        y < 7,
        [remote(mine, mine, n1_s.at[d], n1_r.at[d], at_y(d)) for d in FAR] + spread(mine_x, jnp.minimum(y, 6)),
        moved_first,
    )
    for d in FAR:
        send(mine_first, mine_first, m2_s.at[d], m2_r.at[d], at_y(d))
    send(mine_first, mine_first, n3_s.at[mine_y], n3_r.at[mine_y], sibling)
    for d in NEAR:
        src = ypeer(NY - d)
        k = x * 7 + src
        send_if(
            src < 7, spread(k, src), functools.partial(arrived, new_block(c, k), n1_s.at[d], n1_r.at[d], at_y(d))
        )
    for d in NEAR:
        k = 28 + ypeer(NY - d)
        here = new_block(c, k)
        arrived(here, m2_s.at[d], m2_r.at[d], at_y(d))
        send(here, here, n3_s.at[k], n3_r.at[k], sibling)
    for r in (0,) + NEAR:
        i = ypeer(NY - r)
        blocks = [(d, xpeer(NX - d) * 7 + i) for d in (1, 3, 2)]
        waits = [remote(new_block(c, k), new_block(c, k), n2_s.at[d, i], n2_r.at[d, i], at_x(d)) for d, k in blocks]
        copies = [remote(new_block(c, k), new_block(c, k), n3_s.at[k], n3_r.at[k], sibling) for d, k in blocks]

        def x_arrived(waits=waits):
            for cp in waits:
                cp.wait_recv()

        send_if(i < 7, copies, x_arrived)

    def add_squares(core, waits):
        def step(k, total):
            if waits:
                arrived(new_block(core, k), n3_s.at[k], n3_r.at[k], sibling)
            block = new_block(core, k)[...].astype(F32)
            return total + block * block

        for kind, (start, stop) in enumerate(((0, 24), (24, 36))):
            squares[kind] = lax.fori_loop(start, stop, step, squares[kind] if waits else jnp.zeros((16, HD), F32))

    add_squares(c, False)
    add_squares(oc, True)
    sum_in = jnp.sum(squares[0], axis=0, keepdims=True)
    sum_out = jnp.sum(squares[1], axis=0, keepdims=True)
    scale_in[...] = scale_in[...] / jnp.sqrt(sum_in / HD + 1e-06)
    scale_out[...] = scale_out[...] / jnp.sqrt(sum_out / FH + 1e-06)

    @pl.when(z == 0)
    def _():
        first.wait()

    after = (lax.rem(z + 1, NZ), x, y, c)
    pl.when(z >= NZ // 2)(finish)

    def piece(g, carry):
        here = pl.ds(pl.multiple_of(g * PIECE, PIECE), PIECE)

        @pl.when(z > 0)
        def _():
            arrived(rows_in.at[here], z_s.at[g], z_r.at[g], after)

        rows32 = rows_in[here, :].astype(F32)
        scale = lax.rsqrt(jnp.mean(rows32 * rows32, axis=-1, keepdims=True) + 1e-06)
        pre = nn((rows32 * gains[...]).astype(BF), new[0:HD, :]) * scale * scale_in[...]
        gate = pre[:, :FH]
        mixed = (gate * jax.nn.sigmoid(gate) * pre[:, FH:]).astype(BF)
        out[here, :] = (rows32 + nn(mixed, new[HD : HD + FH, :]) * scale_out[...]).astype(BF)

        @pl.when(z < NZ - 1)
        def _():
            remote(out.at[here], rows_in.at[here], z_s.at[g], z_r.at[g], after).start()

        return carry

    lax.fori_loop(0, GROUPS, piece, 0)

    pl.when(z < NZ // 2)(finish)

    @pl.when(z < NZ - 1)
    def _():
        def left(g, carry):
            here = pl.ds(pl.multiple_of(g * PIECE, PIECE), PIECE)
            remote(out.at[here], rows_in.at[here], z_s.at[g], z_r.at[g], after).wait_send()
            return carry

        lax.fori_loop(0, GROUPS, left, 0)


def per_device(inputs, keys, values, rates, gains, w_in, w_out):
    c_in, c_out, p_f, p_w, p_jt = constants()
    vm = pl.BlockSpec(memory_space=pltpu.VMEM)
    hb = pl.BlockSpec(memory_space=pltpu.HBM)
    V = pltpu.VMEM
    D = pltpu.SemaphoreType.DMA
    scratch = [
        V((6, 2, HD), BF), V((12, FH), BF), V((1, ROWS), F32), V((1, HD), F32),
        V((48, 64), BF), V((48, 64), BF), V((FH, FH), BF),
        V((ROWS, HD), BF), V((ROWS, HD), BF), V((HD, HD), BF), V((HD, HD), BF), V((ROWS, HD), BF), V((16, HD), F32),
        V((NY, 16, HD), BF), V((NX, 16, FH), BF), V((16, 48, HD), BF), V((16, 48, FH), BF),
        V((HD, ROWS), BF), V((HD, ROWS), BF), V((HD, ROWS), BF), V((FH, ROWS), F32), V((2, FH, ROWS), BF),
        V((FH, ROWS), BF),
        V((576, HD), BF), V((576, HD), BF), V((576, HD), F32), V((NX, 7, 16, HD), BF), V((NX, 7, 16, HD), BF),
        V((NY, 16, HD), BF), V((NY, 16, HD), BF), V((NY, 16, HD), BF), V((NY, 16, HD), BF),
        V((16, HD), BF), V((NX, 16, HD), BF), V((16, HD), F32), V((16, HD), F32), V((16, HD), F32),
        V((16, HD), F32), V((16, HD), F32),
        V((HD + FH, HD), BF), V((2, 16, HD), F32),
        D((12,)),
        D((NY,)), D((NY,)), D((NX,)), D((NX,)), D((2, NX)), D((2, NX)), D((NY,)), D((NY,)),
        D((2, NX)), D((2, NX)), D((NY,)), D((NY,)),
        D((5,)), D((5,)), D((NX, NY)), D((NX, NY)), D((NY,)), D((NY,)), D((NY,)), D((NY,)), D((NX,)), D((NX,)),
        D((NY,)), D((NY,)), D((NY,)), D((NY,)), D((NX, NY)), D((NX, NY)), D((36,)), D((36,)),
        D((GROUPS,)), D((GROUPS,)),
    ]
    result = pl.pallas_call(
        kernel,
        out_shape=jax.ShapeDtypeStruct((ROWS, HD), BF),
        in_specs=[hb] * 12,
        out_specs=vm,
        scratch_shapes=scratch,
        compiler_params=pltpu.CompilerParams(
            collective_id=0, has_side_effects=True, vmem_limit_bytes=63 * 2**20
        ),
        cost_estimate=pl.CostEstimate(flops=1500000000, bytes_accessed=6000000, transcendentals=400000),
    )(w_in, w_out, rates, gains, c_in, c_out, p_f, keys, values, inputs, p_w, p_jt)
    return result[None]


def solution(mesh):
    split = Mesh(
        mesh.devices.reshape(mesh.shape["segment"], NX, NY, NC), ("segment", "tok_0", "tok_1", "tok_2")
    )
    in_specs = (
        P(TOK, None),
        P("segment", TOK, None),
        P("segment", TOK, None),
        P("segment", TOK),
        P("segment", None),
        P("segment", TOK, None, None),
        P("segment", TOK, None),
    )
    return jax.shard_map(
        per_device, mesh=split, in_specs=in_specs, out_specs=P("segment", TOK, None), check_vma=False
    )
```

```python
import functools

import jax
import jax.numpy as jnp
import numpy as np
from jax import lax
from jax.experimental import pallas as pl
from jax.experimental.pallas import tpu as pltpu
from jax.sharding import Mesh
from jax.sharding import PartitionSpec as P

NX, NY, NC, NZ = 4, 8, 2, 8
TOK = ("tok_0", "tok_1", "tok_2")
MESH = pl.DeviceIdType.MESH
F32 = jnp.float32
BF = jnp.bfloat16
HD, FH, ROWS = 768, 384, 256
PIECE = 16
GROUPS = ROWS // PIECE


def constants():
    c_in = np.zeros((48, 64), np.float32)
    for half in range(2):
        for y in range(4):
            for r in range(6):
                c_in[half * 24 + y * 6 + r, y * 16 + r * 2 + half] = 1
    c_out = np.zeros((48, 64), np.float32)
    for x in range(NX):
        for r in range(12):
            c_out[x * 12 + r, x * 16 + r] = 1
    p_f = np.zeros((FH, FH), np.float32)
    for c in range(NC):
        for x in range(NX):
            for y in range(NY):
                for r in range(6):
                    p_f[((x * NY + y) * NC + c) * 6 + r, (c * NX + x) * 48 + y * 6 + r] = 1
    p_w = np.zeros((HD, HD), np.float32)
    for b in range(16):
        for half in range(2):
            for r in range(24):
                p_w[b * 48 + half * 24 + r, half * FH + b * 24 + r] = 1
    p_jt = np.zeros((HD, HD), np.float32)
    for c in range(NC):
        for x in range(NX):
            for y in range(NY):
                for r in range(12):
                    p_jt[(c * NY + y) * 48 + x * 12 + r, ((x * NY + y) * NC + c) * 12 + r] = 1
    return [jnp.asarray(a, BF) for a in (c_in, c_out, p_f, p_w, p_jt)]


def nt(a, b):
    return lax.dot_general(a, b, (((1,), (1,)), ((), ())), preferred_element_type=F32)


def nn(a, b):
    return lax.dot_general(a, b, (((1,), (0,)), ((), ())), preferred_element_type=F32)


def tn(a, b):
    return lax.dot_general(a, b, (((0,), (0,)), ((), ())), preferred_element_type=F32)


def parts(a):
    high = a.astype(BF)
    return high, (a - high.astype(F32)).astype(BF)


def row_squares(w):
    squared = w.astype(F32) * w.astype(F32)
    return nt(jnp.ones((16, w.shape[1]), BF), squared.astype(BF))


def moved_by(a, matrix):
    high, low = parts(a)
    return nn(high, matrix) + nn(low, matrix)


NEAR = (1, 7, 2, 6, 3, 5, 4)
FAR = (4, 3, 5, 2, 6, 1, 7)
STEPS = (4, 3, 5, 2, 6, 1, 7, 0)


def kernel(
    win_h, wout_h, rates_h, gains_h, cin_h, cout_h, pf_h, keys_h, vals_h, inputs_h, pw_h, pjt_h,
    out,
    win_own, wout_own, rates, gains, c_in, c_out, p_f, keys, vals, p_w, pjt, rows_in, pad32,
    winpad, woutpad, win, wout,
    keys_t, target_t, targetp_t, dact_t, dhid_t, act_t,
    gs, gr, half, hx_s, hx_r, hy_s, hy_r, ky_s, ky_r, kx_s, kx_r, own_sum, base_x, base_y, scale_in, scale_out,
    new, squares,
    lsem, ya_s, ya_r, xa_s, xa_r, xb_s, xb_r, yb_s, yb_r, cb_s, cb_r, cc_s, cc_r,
    rc_s, rc_r, rx_s, rx_r, ry_s, ry_r, rky_s, rky_r, rkx_s, rkx_r,
    n1_s, n1_r, m2_s, m2_r, n2_s, n2_r, n3_s, n3_r,
    z_s, z_r,
):
    z = lax.axis_index("segment")
    x = lax.axis_index("tok_0")
    y = lax.axis_index("tok_1")
    c = lax.axis_index("tok_2")
    oc = 1 - c

    def ypeer(d):
        return lax.rem(y + d, NY)

    def xpeer(d):
        return lax.rem(x + d, NX)

    def at_y(d):
        return (z, x, ypeer(d), c)

    def at_x(d):
        return (z, xpeer(d), y, c)

    sibling = (z, x, y, oc)
    later = []

    def remote(src, dst, ss, rs, dev):
        return pltpu.make_async_remote_copy(
            src_ref=src, dst_ref=dst, send_sem=ss, recv_sem=rs, device_id=dev, device_id_type=MESH
        )

    def send(src, dst, ss, rs, dev):
        cp = remote(src, dst, ss, rs, dev)
        cp.start()
        later.append(cp.wait_send)

    def send_if(cond, copies, before=None):
        @pl.when(cond)
        def _():
            if before is not None:
                before()
            for cp in copies:
                cp.start()

        @later.append
        @functools.partial(functools.partial, pl.when(cond))
        def _():
            for cp in copies:
                cp.wait_send()

    def finish():
        for wait in later:
            wait()

    def arrived(dst, ss, rs, dev):
        remote(dst, dst, ss, rs, dev).wait_recv()

    pairs = (
        (win_h.at[0], win_own), (wout_h.at[0], wout_own), (pf_h, p_f), (vals_h.at[0], vals), (rates_h, rates),
        (pjt_h, pjt), (cin_h, c_in), (cout_h, c_out), (keys_h.at[0], keys), (pw_h, p_w), (gains_h, gains),
    )
    local = [pltpu.make_async_copy(s, d, lsem.at[i]) for i, (s, d) in enumerate(pairs)]
    for cp in local[:3]:
        cp.start()
    first = pltpu.make_async_copy(inputs_h, rows_in, lsem.at[len(pairs)])

    bar = pltpu.get_barrier_semaphore()
    for d in range(1, NY):
        pl.semaphore_signal(bar, inc=1, device_id=at_y(d), device_id_type=MESH)
    for d in range(1, NX):
        pl.semaphore_signal(bar, inc=1, device_id=at_x(d), device_id_type=MESH)
    pl.semaphore_signal(bar, inc=1, device_id=sibling, device_id_type=MESH)
    for d in (1, NZ - 1):
        pl.semaphore_signal(bar, inc=1, device_id=(lax.rem(z + d, NZ), x, y, c), device_id_type=MESH)
    pad32[...] = jnp.zeros_like(pad32)
    local[0].wait()
    for r in range(6):
        pad32[2 * r : 2 * r + 2, :] = win_own[r].astype(F32)
    winpad[y] = pad32[...].astype(BF)
    pl.semaphore_wait(bar, NY - 1 + NX - 1 + 1 + 2)

    group = y // 4
    place = y - group * 4

    def in_group(g, d):
        return g * 4 + lax.rem(place + d, 4)

    for g, ds in ((group, (2, 1, 3)), (1 - group, (0, 2, 1, 3))):
        for d in ds:
            to = in_group(g, d)
            send(winpad.at[y], winpad.at[y], ya_s.at[to], ya_r.at[y], (z, x, to, c))
    local[1].wait()
    pad32[0:12, 0:FH] = wout_own[...].astype(F32)
    local[2].wait()
    woutpad[x] = nn(pad32[:, 0:FH].astype(BF), p_f[...]).astype(BF)
    for d in range(1, NX):
        send(woutpad.at[x], woutpad.at[x], xa_s.at[d], xa_r.at[d], at_x(d))
    for cp in local[3:]:
        cp.start()

    @pl.when(z == 0)
    def _():
        first.start()

    for cp in local[3:]:
        cp.wait()
    for d in range(1, NX):
        arrived(woutpad.at[xpeer(NX - d)], xa_s.at[d], xa_r.at[d], at_x(d))
    mine_o = c * NY + y
    wout[mine_o] = nn(c_out[...], woutpad[...].reshape(64, FH)).astype(BF)
    for d in FAR:
        send(wout.at[mine_o], wout.at[mine_o], yb_s.at[d], yb_r.at[d], at_y(d))
    send(wout.at[mine_o], wout.at[mine_o], cc_s.at[0], cc_r.at[0], sibling)
    target_t[...] = (vals[...].astype(F32).T * rates[...]).astype(BF)
    for n, (g, ds) in enumerate(((group, (1, 3, 2)), (1 - group, (0, 1, 3, 2)))):
        for d in ds:
            src = in_group(g, d)
            arrived(winpad.at[src], ya_s.at[src], ya_r.at[src], (z, x, src, c))
        mine_i = (c * NX + x) * 2 + g
        win[mine_i] = nn(c_in[...], winpad[pl.ds(g * 4, 4)].reshape(64, HD)).astype(BF)
        for d in (2, 1, 3):
            send(win.at[mine_i], win.at[mine_i], xb_s.at[n, d], xb_r.at[n, d], at_x(d))
        send(win.at[mine_i], win.at[mine_i], cb_s.at[n, 0], cb_r.at[n, 0], sibling)
        if n == 0:
            targetp_t[...] = nn(pjt[...], target_t[...]).astype(BF)
    keys_t[...] = keys[...].astype(F32).T.astype(BF)

    def win_slot(core, d, n):
        return win.at[(core * NX + xpeer(NX - d)) * 2 + (group if n == 0 else 1 - group)]

    for d in NEAR:
        slot = wout.at[c * NY + ypeer(NY - d)]
        arrived(slot, yb_s.at[d], yb_r.at[d], at_y(d))
        send(slot, slot, cc_s.at[d], cc_r.at[d], sibling)
    def x_arrivals(n):
        for d in (1, 3, 2):
            slot = win_slot(c, d, n)
            arrived(slot, xb_s.at[n, d], xb_r.at[n, d], at_x(d))
            send(slot, slot, cb_s.at[n, d], cb_r.at[n, d], sibling)

    x_arrivals(0)
    for d in range(NY):
        arrived(wout.at[oc * NY + ypeer(NY - d)], cc_s.at[d], cc_r.at[d], sibling)
    dact_t[...] = tn(wout[...].reshape(HD, FH), targetp_t[...])
    x_arrivals(1)

    def block(b, carry):
        hidden = nt(win[pl.ds(b * 2, 2)].reshape(96, HD), keys[...]).reshape(2, 2, 24, ROWS)
        gate = hidden[:, 0].reshape(48, ROWS)
        up = hidden[:, 1].reshape(48, ROWS)
        sig = jax.nn.sigmoid(gate)
        silu = gate * sig
        here = pl.ds(pl.multiple_of(b * 48, 16), 48)
        act_t[here, :] = (silu * up).astype(BF)
        da = dact_t[here, :]
        dhid_t[0, here, :] = (da * up * (sig * (1.0 + gate * (1.0 - sig)))).astype(BF)
        dhid_t[1, here, :] = (da * silu).astype(BF)
        return carry

    lax.fori_loop(c * NX, c * NX + NX, block, 0)
    for n in range(2):
        for d in range(NX):
            arrived(win_slot(oc, d, n), cb_s.at[n, d], cb_r.at[n, d], sibling)
    lax.fori_loop(oc * NX, oc * NX + NX, block, 0)

    def out_part(core):
        return nt(act_t[pl.ds(pl.multiple_of(core * 192, 64), 192), :], target_t[...])

    def in_part(core):
        return nt(keys_t[pl.ds(pl.multiple_of(core * FH, FH), FH), :], dhid_t[...].reshape(HD, ROWS))

    def x_rows(d):
        return pl.ds(pl.multiple_of(xpeer(d) * 112, 16), 112)

    y_part = pl.ds(448, 128)
    gs[384:576, :] = out_part(oc).astype(BF)
    send(gs.at[y_part], gr.at[y_part], rc_s.at[4], rc_r.at[4], sibling)
    gs[0:384, :] = in_part(oc).astype(BF)
    for d in (2, 1, 3, 0):
        send(gs.at[x_rows(d)], gr.at[x_rows(d)], rc_s.at[d], rc_r.at[d], sibling)
    half[384:576, :] = out_part(c)
    half[0:384, :] = in_part(c)

    arrived(gr.at[y_part], rc_s.at[4], rc_r.at[4], sibling)
    for k in range(8):
        here = pl.ds(448 + k * 16, 16)
        total = half[here, :] + gr[here, :].astype(F32)
        half[here, :] = total
        hy_s[k] = total.astype(BF)
    for d in FAR:
        send(hy_s.at[ypeer(d)], hy_r.at[y], ry_s.at[d], ry_r.at[d], at_y(d))
    for d in (2, 1, 3, 0):
        arrived(gr.at[x_rows(d)], rc_s.at[d], rc_r.at[d], sibling)
        total = half[x_rows(d), :] + gr[x_rows(d), :].astype(F32)
        if d:
            hx_s[xpeer(d)] = total.reshape(7, 16, HD).astype(BF)
        else:
            half[x_rows(0), :] = total
    for r in STEPS:
        i = ypeer(r)
        send_if(i < 7, [
            remote(hx_s.at[xpeer(d), i], hx_r.at[x, i], rx_s.at[d, i], rx_r.at[d, i], at_x(d)) for d in (2, 1, 3)
        ])

    def row_of(core, k):
        return pl.multiple_of(k * 16 + core * 384 + lax.div(k * 11, 256) * (384 - core * 192), 16)

    lane_in = lax.broadcasted_iota(jnp.int32, (16, HD), 1) - lax.broadcasted_iota(jnp.int32, (16, HD), 0)
    lane_out = lax.broadcasted_iota(jnp.int32, (16, FH), 1) - lax.broadcasted_iota(jnp.int32, (16, FH), 0)

    def base_block(k, ref):
        @pl.when(k < 24)
        def _():
            pick = jnp.where(lane_in == row_of(c, k), 1.0, 0.0).astype(BF)
            ref[...] = nn(nt(pick, win[...].reshape(HD, HD)).astype(BF), p_w[...])

        @pl.when(k >= 24)
        def _():
            pick = jnp.where(lane_out == row_of(c, k) - HD, 1.0, 0.0).astype(BF)
            ref[...] = nn(nt(pick, wout[...].reshape(HD, FH)).astype(BF), pjt[...])

    mine_x = x * 7 + jnp.minimum(y, 6)
    mine_y = 28 + y
    base_block(mine_x, base_x)
    base_block(mine_y, base_y)
    scale_in[...] = jnp.sqrt(moved_by(row_squares(win[...].reshape(HD, HD)), p_w[...]) / HD + 1e-06)

    def reduce_step(r):
        i = ypeer(r)

        def reduced():
            total = half[pl.ds(pl.multiple_of(x * 112 + i * 16, 16), 16), :]
            for d in (1, 3, 2):
                src = xpeer(NX - d)
                arrived(hx_r.at[src, i], rx_s.at[d, i], rx_r.at[d, i], at_x(d))
                total = total + hx_r[src, i].astype(F32)
            if r:
                ky_s[i] = total.astype(BF)
            else:
                own_sum[...] = total

        if r:
            send_if(i < 7, [remote(ky_s.at[i], ky_r.at[y], rky_s.at[r], rky_r.at[r], at_y(r))], reduced)
        else:
            pl.when(i < 7)(reduced)

    for r in STEPS[:4]:
        reduce_step(r)
    total = half[pl.ds(pl.multiple_of(448 + y * 16, 16), 16), :]
    for d in NEAR:
        src = ypeer(NY - d)
        arrived(hy_r.at[src], ry_s.at[d], ry_r.at[d], at_y(d))
        total = total + hy_r[src].astype(F32)
    kx_s[...] = total.astype(BF)
    for d in (2, 1, 3):
        send(kx_s, kx_r.at[x], rkx_s.at[d], rkx_r.at[d], at_x(d))
    base_y[...] = base_y[...] + total
    scale_out[...] = jnp.sqrt(moved_by(row_squares(wout[...].reshape(HD, FH)), pjt[...]) / FH + 1e-06)
    for r in STEPS[4:]:
        reduce_step(r)


    def new_block(core, k):
        return new.at[pl.ds(row_of(core, k), 16)]

    moved = base_y[...]
    for d in (1, 3, 2):
        src = xpeer(NX - d)
        arrived(kx_r.at[src], rkx_s.at[d], rkx_r.at[d], at_x(d))
        moved = moved + kx_r[src].astype(F32)
    mine = new_block(c, mine_y)
    mine[...] = moved.astype(BF)

    mine_first = mine
    mine = new_block(c, mine_x)

    def moved_first():
        moved = base_x[...] + own_sum[...]
        for d in NEAR:
            src = ypeer(NY - d)
            arrived(ky_r.at[src], rky_s.at[d], rky_r.at[d], at_y(d))
            moved = moved + ky_r[src].astype(F32)
        mine[...] = moved.astype(BF)

    def spread(k, i):
        here = new_block(c, k)
        copies = [remote(here, here, n2_s.at[d, i], n2_r.at[d, i], at_x(d)) for d in (2, 1, 3)]
        return copies + [remote(here, here, n3_s.at[k], n3_r.at[k], sibling)]

    send_if(
        y < 7,
        [remote(mine, mine, n1_s.at[d], n1_r.at[d], at_y(d)) for d in FAR] + spread(mine_x, jnp.minimum(y, 6)),
        moved_first,
    )
    for d in FAR:
        send(mine_first, mine_first, m2_s.at[d], m2_r.at[d], at_y(d))
    send(mine_first, mine_first, n3_s.at[mine_y], n3_r.at[mine_y], sibling)
    for d in NEAR:
        src = ypeer(NY - d)
        k = x * 7 + src
        send_if(
            src < 7, spread(k, src), functools.partial(arrived, new_block(c, k), n1_s.at[d], n1_r.at[d], at_y(d))
        )
    for d in NEAR:
        k = 28 + ypeer(NY - d)
        here = new_block(c, k)
        arrived(here, m2_s.at[d], m2_r.at[d], at_y(d))
        send(here, here, n3_s.at[k], n3_r.at[k], sibling)
    for r in (0,) + NEAR:
        i = ypeer(NY - r)
        blocks = [(d, xpeer(NX - d) * 7 + i) for d in (1, 3, 2)]
        waits = [remote(new_block(c, k), new_block(c, k), n2_s.at[d, i], n2_r.at[d, i], at_x(d)) for d, k in blocks]
        copies = [remote(new_block(c, k), new_block(c, k), n3_s.at[k], n3_r.at[k], sibling) for d, k in blocks]

        def x_arrived(waits=waits):
            for cp in waits:
                cp.wait_recv()

        send_if(i < 7, copies, x_arrived)

    def add_squares(core, waits):
        def step(k, total):
            if waits:
                arrived(new_block(core, k), n3_s.at[k], n3_r.at[k], sibling)
            block = new_block(core, k)[...].astype(F32)
            return total + block * block

        for kind, (start, stop) in enumerate(((0, 24), (24, 36))):
            squares[kind] = lax.fori_loop(start, stop, step, squares[kind] if waits else jnp.zeros((16, HD), F32))

    add_squares(c, False)
    add_squares(oc, True)
    sum_in = jnp.sum(squares[0], axis=0, keepdims=True)
    sum_out = jnp.sum(squares[1], axis=0, keepdims=True)
    scale_in[...] = scale_in[...] / jnp.sqrt(sum_in / HD + 1e-06)
    scale_out[...] = scale_out[...] / jnp.sqrt(sum_out / FH + 1e-06)

    @pl.when(z == 0)
    def _():
        first.wait()

    after = (lax.rem(z + 1, NZ), x, y, c)
    pl.when(z >= NZ // 2)(finish)

    def piece(g, carry):
        here = pl.ds(pl.multiple_of(g * PIECE, PIECE), PIECE)

        @pl.when(z > 0)
        def _():
            arrived(rows_in.at[here], z_s.at[g], z_r.at[g], after)

        rows32 = rows_in[here, :].astype(F32)
        scale = lax.rsqrt(jnp.mean(rows32 * rows32, axis=-1, keepdims=True) + 1e-06)
        pre = nn((rows32 * gains[...]).astype(BF), new[0:HD, :]) * scale * scale_in[...]
        gate = pre[:, :FH]
        mixed = (gate * jax.nn.sigmoid(gate) * pre[:, FH:]).astype(BF)
        out[here, :] = (rows32 + nn(mixed, new[HD : HD + FH, :]) * scale_out[...]).astype(BF)

        @pl.when(z < NZ - 1)
        def _():
            remote(out.at[here], rows_in.at[here], z_s.at[g], z_r.at[g], after).start()

        return carry

    lax.fori_loop(0, GROUPS, piece, 0)

    pl.when(z < NZ // 2)(finish)

    @pl.when(z < NZ - 1)
    def _():
        def left(g, carry):
            here = pl.ds(pl.multiple_of(g * PIECE, PIECE), PIECE)
            remote(out.at[here], rows_in.at[here], z_s.at[g], z_r.at[g], after).wait_send()
            return carry

        lax.fori_loop(0, GROUPS, left, 0)


def per_device(inputs, keys, values, rates, gains, w_in, w_out):
    c_in, c_out, p_f, p_w, p_jt = constants()
    vm = pl.BlockSpec(memory_space=pltpu.VMEM)
    hb = pl.BlockSpec(memory_space=pltpu.HBM)
    V = pltpu.VMEM
    D = pltpu.SemaphoreType.DMA
    scratch = [
        V((6, 2, HD), BF), V((12, FH), BF), V((1, ROWS), F32), V((1, HD), F32),
        V((48, 64), BF), V((48, 64), BF), V((FH, FH), BF),
        V((ROWS, HD), BF), V((ROWS, HD), BF), V((HD, HD), BF), V((HD, HD), BF), V((ROWS, HD), BF), V((16, HD), F32),
        V((NY, 16, HD), BF), V((NX, 16, FH), BF), V((16, 48, HD), BF), V((16, 48, FH), BF),
        V((HD, ROWS), BF), V((HD, ROWS), BF), V((HD, ROWS), BF), V((FH, ROWS), F32), V((2, FH, ROWS), BF),
        V((FH, ROWS), BF),
        V((576, HD), BF), V((576, HD), BF), V((576, HD), F32), V((NX, 7, 16, HD), BF), V((NX, 7, 16, HD), BF),
        V((NY, 16, HD), BF), V((NY, 16, HD), BF), V((NY, 16, HD), BF), V((NY, 16, HD), BF),
        V((16, HD), BF), V((NX, 16, HD), BF), V((16, HD), F32), V((16, HD), F32), V((16, HD), F32),
        V((16, HD), F32), V((16, HD), F32),
        V((HD + FH, HD), BF), V((2, 16, HD), F32),
        D((12,)),
        D((NY,)), D((NY,)), D((NX,)), D((NX,)), D((2, NX)), D((2, NX)), D((NY,)), D((NY,)),
        D((2, NX)), D((2, NX)), D((NY,)), D((NY,)),
        D((5,)), D((5,)), D((NX, NY)), D((NX, NY)), D((NY,)), D((NY,)), D((NY,)), D((NY,)), D((NX,)), D((NX,)),
        D((NY,)), D((NY,)), D((NY,)), D((NY,)), D((NX, NY)), D((NX, NY)), D((36,)), D((36,)),
        D((GROUPS,)), D((GROUPS,)),
    ]
    result = pl.pallas_call(
        kernel,
        out_shape=jax.ShapeDtypeStruct((ROWS, HD), BF),
        in_specs=[hb] * 12,
        out_specs=vm,
        scratch_shapes=scratch,
        compiler_params=pltpu.CompilerParams(
            collective_id=0, has_side_effects=True, vmem_limit_bytes=63 * 2**20
        ),
        cost_estimate=pl.CostEstimate(flops=1500000000, bytes_accessed=6000000, transcendentals=400000),
    )(w_in, w_out, rates, gains, c_in, c_out, p_f, keys, values, inputs, p_w, p_jt)
    return result[None]


def solution(mesh):
    split = Mesh(
        mesh.devices.reshape(mesh.shape["segment"], NX, NY, NC), ("segment", "tok_0", "tok_1", "tok_2")
    )
    in_specs = (
        P(TOK, None),
        P("segment", TOK, None),
        P("segment", TOK, None),
        P("segment", TOK),
        P("segment", None),
        P("segment", TOK, None, None),
        P("segment", TOK, None),
    )
    return jax.shard_map(
        per_device, mesh=split, in_specs=in_specs, out_specs=P("segment", TOK, None), check_vma=False
    )
```
